128 devices in a mesh: tile: 64 (over x, y_hi, z, core), sub: 2 (over y_lo).
Axes of the slice: x: 4, y: 4 (y_hi: 2, y_lo: 2; y = y_hi * 2 + y_lo), z: 4, core: 2. Of those that a mesh axis runs over, the one named last changes fastest.
Arguments:
- pulses: bfloat16 [2, 64, 2, 64, 8192], P('sub', 'tile'), may hold values from -6 to 6
- kernel: bfloat16 [262144, 1024], P('tile'), may hold values from -0.1875 to 0.1875
- band_start: int32 [64, 1024], P('tile'), may hold values from 0 to 2048
- band_width: int32 [64, 1024], P('tile'), may hold values from 1 to 2048
- offset: int32 [64], P('tile'), may hold values from 0 to 4096
- owner: int32 [8], replicated, may hold values from 0 to 63, as said below
- angle: float32 [2, 8, 64, 65536], P('sub', None, None, 'tile'), may hold values from -3.140625 to 3.140625
- dest: int32 [4096, 1], P('tile'), may hold values from 0 to 63; in each aligned block of 64 rows (0 to 63, 64 to 127, ...) at most 2 rows name the same one
Outputs:
- merged: float32 [2, 1024, 1024], P(None, 'tile')
The draws below stay inside these ranges and needn't reach their ends.
Inputs may be any that keep to these rules, and one draw needn't show every extreme that they name: `owner`: 8 different tile indices, among them the first and the last tile. `dest`: among the 64 strips of one tile, no parent tile is named more than 2 times.
All inputs are finite; a program needn't handle non-finite values.
Results may differ from the reference program's by a relative error of at most 0.0037.
Values may be sent and summed in bfloat16 or wider, within the bound.
No kernel may reach another device: no remote copies, remote signals or barrier semaphores. Data moves between devices by JAX's collectives and lax.ppermute only.
A program may use at most 192 MiB of HBM per device.

```python
import math
import jax
import jax.numpy as jnp
import numpy as np
from jax import lax

R = 8192
P_SIZE = 64
WIN = 4096
BAND = 2048
PIX_R = 1024
STRIP = 16
CAP = 2
STEPS = 8
PIX_A = 1024
N_TILE = 64
N_SUB = 2


def draw_owner(key, part):
    key = jax.random.fold_in(key, 7)
    pick_key = jax.random.fold_in(key, 1)
    order_key = jax.random.fold_in(key, 2)
    middle = jax.random.permutation(pick_key, N_TILE - 2)[:STEPS - 2].astype(jnp.int32) + 1
    ends = jnp.array([0, N_TILE - 1], dtype=jnp.int32)
    chosen = jnp.concatenate([ends, middle])
    return jax.random.permutation(order_key, chosen).astype(jnp.int32)


def place_ends(values, rng, smallest, top_value):
    place = [jax.random.randint(jax.random.fold_in(rng, axis), (), 0, length) for axis, length in enumerate(values.shape)]
    longest = values.shape.index(max(values.shape))
    next_to = place[:longest] + [(place[longest] + 1) % values.shape[longest]] + place[longest + 1:]
    return values.at[tuple(place)].set(smallest).at[tuple(next_to)].set(top_value)


def steps_of(key, shape, shards, smallest, top_value):
    def one(dim, shards_of):
        draws = jax.random.uniform(jax.random.fold_in(jax.random.fold_in(key, 6), dim), (shards_of,), jnp.float32, smallest / len(shards), top_value / len(shards))
        return jnp.repeat(jnp.exp(draws), shape[dim] // shards_of).reshape((-1,) + (1,) * (len(shape) - dim - 1))

    level = one(*shards[0])
    for cut in shards[1:]:
        level = level * one(*cut)
    return level


def assign_block(rng, own, number, rows, count, top, limit, lean):
    order = jax.random.permutation(rng, count)
    heavy_load, usual = portions_of(count, rows * top, limit, lean, True), portions_of(count, rows * top, limit, lean, False)
    places = jnp.arange(count)

    def named(lengths, turn):
        used = int((lengths > 0).sum())
        fixed = max(1, used // 4)
        moved = fixed + (places - fixed + turn * (used - fixed)) % max(1, count - fixed)
        return jnp.zeros((count,), jnp.int32).at[order[jnp.where(places < fixed, places, moved)]].set(jnp.asarray(lengths, jnp.int32))

    lengths = jnp.where(number % 4 == 0, named(heavy_load, number // 4), named(usual, number - number // 4 - 1))
    mixed = jax.random.permutation(jax.random.fold_in(own, 3), count)
    donor, taker = mixed[0:count // 2 * 2:2], mixed[1:count // 2 * 2:2]
    slack = jnp.minimum(lengths[donor] - 1, limit - lengths[taker]) // 2
    slack = jnp.where((donor == order[0]) | (taker == order[0]) | (lengths[taker] == 0), 0, jnp.maximum(slack, 0))
    moved = jax.random.randint(jax.random.fold_in(own, 4), (count // 2,), 0, 1 << 20) % (slack + 1)
    lengths = lengths.at[donor].add(-moved).at[taker].add(moved)
    labels = jnp.searchsorted(jnp.cumsum(lengths), jnp.arange(rows * top), side="right").astype(jnp.int32)
    listing = labels.reshape(top, rows).T
    listing = listing[jax.random.permutation(jax.random.fold_in(own, 1), rows)]
    turn = jax.random.randint(jax.random.fold_in(own, 2), (rows, 1), 0, top)
    return jnp.take_along_axis(listing, (jnp.arange(top)[None, :] + turn) % top, axis=1)


def portions_of(count, total, most, skew, full):
    weights = [(1 << 20) // math.isqrt(grade ** skew) + 1 for grade in range(1, count + 1)]
    largest = most if full else min(most, max(-(-total // count), total * weights[0] // sum(weights)))
    least = 1 if total - largest >= count - 1 else 0
    given, rest = [largest] + [least] * (count - 1), total - largest - least * (count - 1)
    while rest > 0:
        free = [i for i in range(1, count) if given[i] < largest] or [i for i in range(1, count) if given[i] < most]
        pool, remaining = sum([weights[i] for i in free]), rest
        for i in free:
            more = min(most - given[i], max(1, remaining * weights[i] // pool), rest)
            given[i] = given[i] + more
            rest = rest - more
    return np.array(given)


def centred(key, extent, width, most, split=(), held_as=jnp.bfloat16):
    factor_of = steps_of(key, extent, split, -0.22, 0.18) if split else 1.0
    entries = jax.random.normal(key, extent, jnp.float32) * width * factor_of
    return jnp.minimum(jnp.maximum(entries, -most), most).astype(held_as)


def setup_inputs(seed: int = 0) -> dict:
    key_list = jax.random.split(jax.random.key(seed), 9)
    pulses = centred(key_list[0], (N_SUB, N_TILE, 2, P_SIZE, R), 1.0, 6.0, ((0, 2), (1, 64)))
    kernel = centred(key_list[1], (N_TILE * WIN, PIX_R), (BAND // 2) ** -0.5, 0.1875, ((0, 64),))
    band_start = place_ends(jax.random.randint(key_list[2], (N_TILE, PIX_R), 0, WIN - BAND + 1), jax.random.fold_in(key_list[2], 1), 0, WIN - BAND).astype(jnp.int32)
    band_width = place_ends(jax.random.randint(key_list[3], (N_TILE, PIX_R), 1, BAND + 1), jax.random.fold_in(key_list[3], 1), 1, BAND).astype(jnp.int32)
    offset = place_ends(jax.random.randint(key_list[4], (N_TILE,), 0, R - WIN + 1), jax.random.fold_in(key_list[4], 1), 0, R - WIN).astype(jnp.int32)
    owner = draw_owner(jax.random.fold_in(key_list[8], 71), 0)
    angle = jnp.clip(jax.random.uniform(key_list[6], (N_SUB, STEPS, P_SIZE, N_TILE * PIX_A), jnp.float32, -3.140625, 3.140625), -3.140625, 3.140625)
    dest_keys = jax.random.split(jax.random.fold_in(key_list[7], 1), (N_TILE * N_TILE) // N_TILE)
    dest_turns = jax.random.permutation(jax.random.fold_in(key_list[7], 3), (N_TILE * N_TILE) // N_TILE)
    dest = jax.vmap(lambda own, number: assign_block(jax.random.fold_in(key_list[7], 2), own, number, N_TILE, N_TILE, 1, CAP, 2))(dest_keys, dest_turns).reshape((N_TILE * N_TILE, 1))
    return {"pulses": pulses, "kernel": kernel, "band_start": band_start, "band_width": band_width, "offset": offset, "owner": owner, "angle": angle, "dest": dest}


def phase_matrix(angle_tile, scale):
    cosine = (jnp.cos(angle_tile) * scale).T
    sine_part = (jnp.sin(angle_tile) * scale).T
    top_rows = jnp.concatenate([cosine, -sine_part], 1)
    low_rows = jnp.concatenate([sine_part, cosine], 1)
    return jnp.concatenate([top_rows, low_rows], 0).astype(jnp.bfloat16)

def reference(pulses, kernel, band_start, band_width, offset, owner, angle, dest):
    phase_gain = 1.0 / math.sqrt(P_SIZE * STEPS * N_SUB)
    kernels = kernel.reshape(N_TILE, WIN, PIX_R)
    depth = jnp.arange(WIN, dtype=jnp.int32)[None, :, None]
    in_band = (depth >= band_start[:, None, :]) & (depth < (band_start + band_width)[:, None, :])
    masked = jnp.where(in_band, kernels, jnp.zeros((), kernels.dtype))
    angles = angle.reshape(N_SUB, STEPS, P_SIZE, N_TILE, PIX_A)

    def tile_image(tile_id):
        subimage = jnp.zeros((2 * PIX_A, PIX_R), jnp.float32)
        for group in range(N_SUB):
            for step in range(STEPS):
                block_data = lax.dynamic_index_in_dim(pulses[group], owner[step], 0, keepdims=False)
                windowed = lax.dynamic_slice_in_dim(block_data, offset[tile_id], WIN, 2).reshape(2 * P_SIZE, WIN)
                interp = jnp.dot(windowed, masked[tile_id], preferred_element_type=jnp.float32).astype(jnp.bfloat16)
                angle_tile = lax.dynamic_index_in_dim(angles[group, step], tile_id, 1, keepdims=False)
                subimage = subimage + jnp.dot(phase_matrix(angle_tile, phase_gain), interp, preferred_element_type=jnp.float32)
        return subimage
    images = lax.map(tile_image, jnp.arange(N_TILE, dtype=jnp.int32))
    strips = images.reshape(N_TILE, 2, N_TILE, STRIP, PIX_R).transpose(0, 2, 1, 3, 4)
    strips = strips.reshape(N_TILE * N_TILE, 2, STRIP, PIX_R)
    summed = jax.ops.segment_sum(strips, dest[:, 0], num_segments=N_TILE)
    merged = summed / math.sqrt(N_TILE)
    return merged.transpose(1, 0, 2, 3).reshape(2, N_TILE * STRIP, PIX_R)
```

```python
import math

import jax
import jax.numpy as jnp
from jax import lax
from jax.experimental import pallas as pl
from jax.experimental.pallas import tpu as pltpu
from jax.sharding import PartitionSpec as P

STRIP = 16
PAD = 256


def mate_of(count):
    return [(i, i ^ 1) for i in range(count)]


def fit_window(kernel, band_start, band_width, shift, rows):
    depth = lax.broadcasted_iota(jnp.int32, (rows, kernel.shape[1]), 0) - shift
    in_band = (depth >= band_start) & (depth < band_start + band_width)
    framed = lax.dynamic_slice_in_dim(
        jnp.pad(kernel, ((PAD, PAD), (0, 0))), PAD - shift, rows, 0
    )
    return jnp.where(in_band, framed, jnp.zeros((), kernel.dtype))


def phase_rows(angle, scale, core):
    steps, pulses, rows = angle.shape
    ordered = angle.reshape(steps, pulses // 2, 2, rows).transpose(2, 1, 0, 3)
    ordered = jnp.where(core == 0, ordered, ordered[::-1])
    cosine = (jnp.cos(ordered) * scale).astype(jnp.bfloat16)
    sine = (jnp.sin(ordered) * scale).astype(jnp.bfloat16)
    top = jnp.stack([cosine, -sine], 2).reshape(2 * steps * pulses, rows)
    low = jnp.stack([sine, cosine], 2).reshape(2 * steps * pulses, rows)
    return jnp.concatenate([top, low], 1).T


def interp_kernel(info, rows_ref, kernel_ref, keep_ref, send_ref, *, depth):
    half, tile = pl.program_id(0), pl.program_id(1)
    start = pl.multiple_of(info[1 + tile], 128)
    out = jnp.dot(
        rows_ref[:, pl.ds(start, depth)], kernel_ref[0], preferred_element_type=jnp.float32
    ).astype(jnp.bfloat16)

    @pl.when(half == 0)
    def _():
        keep_ref[...] = out

    @pl.when(half == 1)
    def _():
        send_ref[...] = out


def interpolate(info, rows, kernels):
    count, samples = rows.shape
    tiles, depth, columns = kernels.shape
    half = columns // 2
    block = 256
    parts = half // block
    out = jax.ShapeDtypeStruct((count, tiles * half), jnp.bfloat16)

    def kernel_at(h, t, n, info):
        return (t, 0, jnp.where(h == 0, info[0], 1 - info[0]) * parts + n)

    def keep_at(h, t, n, info):
        return (0, jnp.where(h == 0, t * parts + n, tiles * parts - 1))

    def send_at(h, t, n, info):
        return (0, jnp.where(h == 0, 0, t * parts + n))

    return pl.pallas_call(
        lambda *refs: interp_kernel(*refs, depth=depth),
        out_shape=(out, out),
        grid_spec=pltpu.PrefetchScalarGridSpec(
            num_scalar_prefetch=1,
            grid=(2, tiles, parts),
            in_specs=[
                pl.BlockSpec((count, samples), lambda h, t, n, info: (0, 0)),
                pl.BlockSpec((1, depth, block), kernel_at),
            ],
            out_specs=[
                pl.BlockSpec((count, block), keep_at),
                pl.BlockSpec((count, block), send_at),
            ],
        ),
        compiler_params=pltpu.CompilerParams(vmem_limit_bytes=56 << 20),
        cost_estimate=pl.CostEstimate(
            flops=2 * count * depth * tiles * columns,
            bytes_accessed=2 * (count * samples + tiles * depth * columns),
            transcendentals=0,
        ),
        name="interp",
    )(info, rows, kernels)


def image_kernel(dest, phase_ref, own_ref, mate_ref, out_ref, total_ref, *, steps):
    tile, part = pl.program_id(0), pl.program_id(1)
    half = out_ref.shape[1]
    near = own_ref.shape[0]
    block = phase_ref.shape[1]

    @pl.when((tile == 0) & (part == 0))
    def _():
        total_ref[...] = jnp.zeros_like(total_ref)

    def add(own_column, mate_column):
        image = jnp.dot(
            phase_ref[0, :, :near],
            own_ref[:, own_column : own_column + half],
            preferred_element_type=jnp.float32,
        ) + jnp.dot(
            phase_ref[0, :, near:],
            mate_ref[:, mate_column : mate_column + half],
            preferred_element_type=jnp.float32,
        )
        per_side = steps // 2
        side = part // per_side
        first = (part % per_side) * (block // STRIP)
        for strip in range(block // STRIP):
            target = dest[tile, first + strip]
            at = pl.multiple_of(target * (2 * STRIP) + side * STRIP, STRIP)
            total_ref[pl.ds(at, STRIP), :] += image[strip * STRIP : (strip + 1) * STRIP]

    @pl.when(tile == 0)
    def _():
        add(0, half)

    @pl.when(tile == 1)
    def _():
        add(half, 0)

    @pl.when((tile == 1) & (part == steps - 1))
    def _():
        out_ref[...] = total_ref[...].astype(out_ref.dtype)


def parent_sums(dest, phases, own, mate):
    tiles, rows, depth = phases.shape
    half = own.shape[1] // 2
    block = 512
    steps = rows // block
    return pl.pallas_call(
        lambda *refs: image_kernel(*refs, steps=steps),
        out_shape=jax.ShapeDtypeStruct((rows, half), jnp.bfloat16),
        grid_spec=pltpu.PrefetchScalarGridSpec(
            num_scalar_prefetch=1,
            grid=(tiles, steps),
            in_specs=[
                pl.BlockSpec((1, block, depth), lambda t, i, dest: (t, i, 0)),
                pl.BlockSpec(own.shape, lambda t, i, dest: (0, 0)),
                pl.BlockSpec(mate.shape, lambda t, i, dest: (0, 0)),
            ],
            out_specs=pl.BlockSpec((rows, half), lambda t, i, dest: (0, 0)),
            scratch_shapes=[pltpu.VMEM((rows, half), jnp.float32)],
        ),
        compiler_params=pltpu.CompilerParams(vmem_limit_bytes=48 << 20),
        cost_estimate=pl.CostEstimate(
            flops=2 * tiles * rows * depth * half,
            bytes_accessed=2 * (tiles * rows * depth + 2 * rows * half),
            transcendentals=0,
        ),
        name="image",
    )(dest, phases, own, mate)


def gather_rows(rows, tile_count):
    groups = [[t for t in range(tile_count) if t % 2 == c] for c in range(2)]
    return lax.all_gather(rows, "tile", axis=0, tiled=True, axis_index_groups=groups)


def local(pulses, kernel, band_start, band_width, offset, owner, angle, dest):
    groups = lax.axis_size("sub")
    tile_count = lax.axis_size("tile")
    core = lax.axis_index("tile") % 2
    mates = mate_of(tile_count)
    _, _, parts, pulse_count, samples = pulses.shape
    step_count = owner.shape[0]
    window, columns = kernel.shape
    depth = window + PAD
    scale = 1.0 / math.sqrt(pulse_count * step_count * groups)

    spread = lax.all_to_all(
        pulses[0, 0].transpose(1, 0, 2), "tile", split_axis=0, concat_axis=0, tiled=True
    )
    mine = jnp.take(spread, owner, axis=0).transpose(1, 0, 2).reshape(parts * step_count, samples)

    small = jnp.concatenate([band_start[0], band_width[0], dest[:, 0], offset])
    other_small = lax.ppermute(small, "tile", mates)
    other_kernel = lax.ppermute(kernel, "tile", mates)
    other_angle = lax.ppermute(angle[0], "tile", mates)

    rows = gather_rows(mine, tile_count)

    starts, framed, phases, dests = [], [], [], []
    for ints, weights, phase in ((small, kernel, angle[0]), (other_small, other_kernel, other_angle)):
        at = ints[-1]
        start = jnp.minimum(at // 128 * 128, samples - depth)
        starts.append(start)
        framed.append(
            fit_window(weights, ints[:columns][None], ints[columns : 2 * columns][None], at - start, depth)
        )
        phases.append(phase_rows(phase, scale, core))
        dests.append(ints[2 * columns : -1])
    info = jnp.stack([core, *starts]).astype(jnp.int32)

    keep, send = interpolate(info, rows, jnp.stack(framed))
    mate = lax.ppermute(send, "tile", mates)
    sums = parent_sums(jnp.stack(dests), jnp.stack(phases), keep, mate)

    received = lax.all_to_all(sums, ("tile", "sub"), split_axis=0, concat_axis=0, tiled=True)
    received = received.reshape(tile_count // 2, 2, groups, STRIP, columns // 2)
    side = jnp.sum(received.astype(jnp.float32), axis=(0, 2)) / math.sqrt(tile_count)
    side = side.transpose(1, 0, 2).reshape(STRIP, columns)
    other = lax.ppermute(side, "sub", [(0, 1), (1, 0)])
    first = lax.axis_index("sub") == 0
    return jnp.stack([jnp.where(first, side, other), jnp.where(first, other, side)])


def solution(mesh):
    placed = (
        P("sub", "tile", None, None, None),
        P("tile", None),
        P("tile", None),
        P("tile", None),
        P("tile"),
        P(),
        P("sub", None, None, "tile"),
        P("tile", None),
    )
    return jax.shard_map(
        local, mesh=mesh, in_specs=placed, out_specs=P(None, "tile", None), check_vma=False
    )
```

```python
import math

import jax
import jax.numpy as jnp
from jax import lax
from jax.experimental import pallas as pl
from jax.experimental.pallas import tpu as pltpu
from jax.sharding import PartitionSpec as P

STRIP = 16
PAD = 256
SIDES = (4, 2, 4, 2)
MIB = 1 << 20
RING = (0, -1, 1, 2)


def tile_at(x, y, z, core):
    return (((x % SIDES[0]) * SIDES[1] + y % SIDES[1]) * SIDES[2] + z % SIDES[2]) * SIDES[3] + core


def shifted(dx=0, dy=0, dz=0):
    return [
        (tile_at(x, y, z, c), tile_at(x + dx, y + dy, z + dz, c))
        for x in range(SIDES[0])
        for y in range(SIDES[1])
        for z in range(SIDES[2])
        for c in range(SIDES[3])
    ]


def mates():
    count = math.prod(SIDES)
    return [(i, i ^ 1) for i in range(count)]


def ring_of_blocks(block, up, down):
    half = block.shape[1] // 2
    below = lax.ppermute(block, "tile", up)
    above = lax.ppermute(block, "tile", down)
    far_left = lax.ppermute(below[:, :half], "tile", up)
    far_right = lax.ppermute(above[:, half:], "tile", down)
    return jnp.concatenate([block, below, above, jnp.concatenate([far_left, far_right], 1)], 0)


def ring_of_lines(line, up, down):
    half = line.shape[0] // 2
    below = lax.ppermute(line, "tile", up)
    above = lax.ppermute(line, "tile", down)
    far_top = lax.ppermute(below[:half], "tile", up)
    far_low = lax.ppermute(above[half:], "tile", down)
    return [line, below, above], [far_top, far_low]


def gather_rows(mine):
    up_x, down_x, up_z, down_z = shifted(dx=1), shifted(dx=-1), shifted(dz=1), shifted(dz=-1)
    other = lax.ppermute(mine, "tile", shifted(dy=1))
    line_a = ring_of_blocks(mine, up_x, down_x)
    line_b = ring_of_blocks(other, up_z, down_z)
    first_a, last_a = ring_of_lines(line_a, up_z, down_z)
    first_b, last_b = ring_of_lines(line_b, up_x, down_x)
    return first_a + first_b, last_a + last_b


def block_order():
    first, last = [], []
    for dy in (0, 1):
        lines = [[(a, dy, b) if dy == 0 else (b, dy, a) for a in RING] for b in RING]
        first += lines[0] + lines[1] + lines[2]
        last += lines[3]
    return first + last


def frame_kernel(info, band_ref, before_ref, now_ref, out_ref):
    step = pl.program_id(0)
    shift = info[0]
    rows, columns = out_ref.shape
    source = lax.broadcasted_iota(jnp.int32, (rows, 2 * rows), 1)
    target = lax.broadcasted_iota(jnp.int32, (rows, 2 * rows), 0)
    move = jnp.where(source == target + (rows - shift), 1.0, 0.0).astype(jnp.bfloat16)
    moved = jnp.dot(move[:, :rows], before_ref[...], preferred_element_type=jnp.float32)
    moved += jnp.dot(move[:, rows:], now_ref[...], preferred_element_type=jnp.float32)
    depth = lax.broadcasted_iota(jnp.int32, (rows, columns), 0) + (step * rows - shift)
    low, high = band_ref[0:1, :], band_ref[1:2, :]
    out_ref[...] = jnp.where((depth >= low) & (depth < high), moved, 0.0).astype(out_ref.dtype)


def fit_window(shift, bands, kernel):
    window, columns = kernel.shape
    count = window // PAD
    rows = window + PAD
    return pl.pallas_call(
        frame_kernel,
        out_shape=jax.ShapeDtypeStruct((rows, columns), kernel.dtype),
        grid_spec=pltpu.PrefetchScalarGridSpec(
            num_scalar_prefetch=1,
            grid=(count + 1,),
            in_specs=[
                pl.BlockSpec((2, columns), lambda i, info: (0, 0)),
                pl.BlockSpec((PAD, columns), lambda i, info: (jnp.maximum(i - 1, 0), 0)),
                pl.BlockSpec((PAD, columns), lambda i, info: (jnp.minimum(i, count - 1), 0)),
            ],
            out_specs=pl.BlockSpec((PAD, columns), lambda i, info: (i, 0)),
        ),
        compiler_params=pltpu.CompilerParams(vmem_limit_bytes=24 * MIB),
        cost_estimate=pl.CostEstimate(
            flops=4 * rows * PAD * columns, bytes_accessed=6 * rows * columns, transcendentals=0
        ),
        name="frame",
    )(shift, bands, kernel, kernel)


def sine_cosine(angle):
    half = angle * 0.5
    square = half * half
    sine, cosine = jnp.float32(-1.0 / math.factorial(11)), jnp.float32(1.0 / math.factorial(12))
    for power in (9, 7, 5, 3, 1):
        sine = sine * square + jnp.float32((-1) ** (power // 2) / math.factorial(power))
    for power in (10, 8, 6, 4, 2, 0):
        cosine = cosine * square + jnp.float32((-1) ** (power // 2) / math.factorial(power))
    sine = sine * half
    return 2.0 * sine * cosine, 1.0 - 2.0 * sine * sine


def phase_kernel(order, angle_ref, out_ref, *, scale):
    pulses, steps, rows = angle_ref.shape
    group = 128 // steps
    for block in range(pulses // group):
        picked = [angle_ref[order[block * group + i]] for i in range(group)]
        sine, cosine = sine_cosine(jnp.concatenate(picked, 0))
        at = block * 128
        out_ref[:, at : at + 128] = (cosine * scale).T.astype(out_ref.dtype)
        at += pulses * steps
        out_ref[:, at : at + 128] = (sine * scale).T.astype(out_ref.dtype)


def phase_rows(order, angle, scale):
    pulses, steps, rows = angle.shape
    depth = 2 * pulses * steps
    block = 128
    return pl.pallas_call(
        lambda *refs: phase_kernel(*refs, scale=scale),
        out_shape=jax.ShapeDtypeStruct((rows, depth), jnp.bfloat16),
        grid_spec=pltpu.PrefetchScalarGridSpec(
            num_scalar_prefetch=1,
            grid=(rows // block,),
            in_specs=[pl.BlockSpec((pulses, steps, block), lambda i, order: (0, 0, i))],
            out_specs=pl.BlockSpec((block, depth), lambda i, order: (i, 0)),
        ),
        compiler_params=pltpu.CompilerParams(vmem_limit_bytes=24 * MIB),
        cost_estimate=pl.CostEstimate(
            flops=20 * depth * rows, bytes_accessed=4 * depth * rows, transcendentals=0
        ),
        name="phases",
    )(order, angle)


def interp_kernel(info, *refs, depth, pieces):
    parts, own_ref, mate_ref = refs[:pieces], refs[pieces], refs[pieces + 1]
    keep_ref, send_ref, rows_ref, sems = refs[pieces + 2 :]
    tile, half, part = pl.program_id(0), pl.program_id(1), pl.program_id(2)
    count = rows_ref.shape[0]

    @pl.when((tile == 0) & (half == 0) & (part == 0))
    def _():
        copies, at = [], 0
        for i, piece in enumerate(parts):
            size = piece.shape[0]
            copies.append(pltpu.make_async_copy(piece, rows_ref.at[pl.ds(at, size)], sems.at[i]))
            at += size
        for copy in copies:
            copy.start()
        for copy in copies:
            copy.wait()

    def work(kernel_ref):
        start = pl.multiple_of(info[1 + tile], 128)
        out = jnp.dot(
            rows_ref[:, pl.ds(start, depth)], kernel_ref[...], preferred_element_type=jnp.float32
        )
        out = out.reshape(count // 16, 2, 8, out.shape[1])
        real = out[:, 0].reshape(count // 2, -1).astype(jnp.bfloat16)
        imag = out[:, 1].reshape(count // 2, -1).astype(jnp.bfloat16)

        @pl.when(half == 0)
        def _():
            keep_ref[0] = real
            keep_ref[1] = imag

        @pl.when(half == 1)
        def _():
            send_ref[0] = real
            send_ref[1] = imag

    @pl.when(tile == 0)
    def _():
        work(own_ref)

    @pl.when(tile == 1)
    def _():
        work(mate_ref)


def interpolate(info, pieces, own, mate):
    count = sum(piece.shape[0] for piece in pieces)
    samples = pieces[0].shape[1]
    depth, columns = own.shape
    half = columns // 2
    block = 256
    parts = half // block
    out = jax.ShapeDtypeStruct((2, count // 2, 2 * half), jnp.bfloat16)

    def column(h, n, info):
        return jnp.where(h == 0, info[0], 1 - info[0]) * parts + n

    def own_at(t, h, n, info):
        return (0, jnp.where(t == 0, column(h, n, info), column(1, parts - 1, info)))

    def mate_at(t, h, n, info):
        return (0, jnp.where(t == 1, column(h, n, info), column(0, 0, info)))

    def keep_at(t, h, n, info):
        return (0, 0, t * parts + jnp.where(h == 0, n, parts - 1))

    def send_at(t, h, n, info):
        return (0, 0, jnp.where(h == 1, t * parts + n, jnp.maximum(t * parts - 1, 0)))

    return pl.pallas_call(
        lambda *refs: interp_kernel(*refs, depth=depth, pieces=len(pieces)),
        out_shape=(out, out),
        grid_spec=pltpu.PrefetchScalarGridSpec(
            num_scalar_prefetch=1,
            grid=(2, 2, parts),
            in_specs=[pl.BlockSpec(memory_space=pl.ANY) for _ in pieces]
            + [pl.BlockSpec((depth, block), own_at), pl.BlockSpec((depth, block), mate_at)],
            out_specs=[
                pl.BlockSpec((2, count // 2, block), keep_at),
                pl.BlockSpec((2, count // 2, block), send_at),
            ],
            scratch_shapes=[
                pltpu.VMEM((count, samples), jnp.bfloat16),
                pltpu.SemaphoreType.DMA((len(pieces),)),
            ],
        ),
        compiler_params=pltpu.CompilerParams(vmem_limit_bytes=40 * MIB),
        cost_estimate=pl.CostEstimate(
            flops=4 * count * depth * columns,
            bytes_accessed=2 * (count * samples + 2 * depth * columns),
            transcendentals=0,
        ),
        name="interp",
    )(info, *pieces, own, mate)


def image_kernel(info, dest, own_phase, mate_phase, *refs, steps):
    kept, taken, (out_ref, rhs_ref, total_ref) = refs[:2], refs[2:4], refs[4:]
    tile, part = pl.program_id(0), pl.program_id(1)
    half = out_ref.shape[1]
    depth = rhs_ref.shape[0]
    core = info[0]

    @pl.when((tile == 0) & (part == 0))
    def _():
        total_ref[...] = jnp.zeros_like(total_ref)

    def lay(pieces, cores_at, column):
        at = 0
        for piece in pieces:
            size = piece.shape[1]
            real = piece[0, :, column : column + half]
            imag = piece[1, :, column : column + half]
            cos_rows = pl.ds(pl.multiple_of(cores_at * (depth // 4) + at, 16), size)
            sin_rows = pl.ds(pl.multiple_of(cores_at * (depth // 4) + at + depth // 2, 16), size)
            rhs_ref[cos_rows, :half] = real
            rhs_ref[sin_rows, :half] = -imag
            rhs_ref[cos_rows, half:] = imag
            rhs_ref[sin_rows, half:] = real
            at += size

    @pl.when((tile == 0) & (part == 0))
    def _():
        lay(kept, core, 0)
        lay(taken, 1 - core, half)

    @pl.when((tile == 1) & (part == 0))
    def _():
        lay(kept, core, half)
        lay(taken, 1 - core, 0)

    def add(phase_ref):
        image = jnp.dot(phase_ref[...], rhs_ref[...], preferred_element_type=jnp.float32)
        block = image.shape[0]
        for strip in range(block // STRIP):
            target = dest[tile, part * (block // STRIP) + strip]
            at = pl.multiple_of(target * (2 * STRIP), 2 * STRIP)
            rows = slice(strip * STRIP, (strip + 1) * STRIP)
            total_ref[pl.ds(at, STRIP), :] += image[rows, :half]
            total_ref[pl.ds(at + STRIP, STRIP), :] += image[rows, half:]

    @pl.when(tile == 0)
    def _():
        add(own_phase)

    @pl.when(tile == 1)
    def _():
        add(mate_phase)

    @pl.when((tile == 1) & (part == steps - 1))
    def _():
        out_ref[...] = total_ref[...].astype(out_ref.dtype)


def parent_sums(info, dest, own_phase, mate_phase, kept, taken):
    rows, depth = own_phase.shape
    half = kept[0].shape[2] // 2
    block = 256
    steps = rows // block
    out_rows = 2 * rows

    def whole(array):
        return pl.BlockSpec(array.shape, lambda t, i, info, dest: (0,) * array.ndim)

    return pl.pallas_call(
        lambda *refs: image_kernel(*refs, steps=steps),
        out_shape=jax.ShapeDtypeStruct((out_rows, half), jnp.bfloat16),
        grid_spec=pltpu.PrefetchScalarGridSpec(
            num_scalar_prefetch=2,
            grid=(2, steps),
            in_specs=[
                pl.BlockSpec(
                    (block, depth), lambda t, i, info, dest: (jnp.where(t == 0, i, steps - 1), 0)
                ),
                pl.BlockSpec((block, depth), lambda t, i, info, dest: (jnp.where(t == 1, i, 0), 0)),
                *[whole(array) for array in (*kept, *taken)],
            ],
            out_specs=pl.BlockSpec((out_rows, half), lambda t, i, info, dest: (0, 0)),
            scratch_shapes=[
                pltpu.VMEM((depth, 2 * half), jnp.bfloat16),
                pltpu.VMEM((out_rows, half), jnp.float32),
            ],
        ),
        compiler_params=pltpu.CompilerParams(vmem_limit_bytes=40 * MIB),
        cost_estimate=pl.CostEstimate(
            flops=8 * rows * depth * half,
            bytes_accessed=4 * rows * depth + 8 * rows * half,
            transcendentals=0,
        ),
        name="image",
    )(info, dest, own_phase, mate_phase, *kept, *taken)


def local(pulses, kernel, band_start, band_width, offset, owner, angle, dest):
    groups = lax.axis_size("sub")
    tile_count = lax.axis_size("tile")
    me = lax.axis_index("tile")
    core = me % SIDES[3]
    _, _, parts, pulse_count, samples = pulses.shape
    step_count = owner.shape[0]
    window, columns = kernel.shape
    depth = window + PAD
    scale = 1.0 / math.sqrt(pulse_count * step_count * groups)

    spread = lax.all_to_all(
        pulses[0, 0].transpose(1, 0, 2), "tile", split_axis=0, concat_axis=0, tiled=True
    )
    mine = jnp.take(spread, owner, axis=0).transpose(1, 0, 2).reshape(parts * step_count, samples)
    first, last = gather_rows(mine)

    start = jnp.minimum(offset[0] // 128 * 128, samples - depth)
    bands = jnp.concatenate([band_start, band_start + band_width], 0)
    own_kernel = fit_window((offset - start).astype(jnp.int32), bands, kernel)
    x, y, z = me // (SIDES[1] * SIDES[2] * SIDES[3]), me // (SIDES[2] * SIDES[3]), me // SIDES[3]
    order = jnp.stack(
        [tile_at(x + dx, y + dy, z + dz, c) for c in range(SIDES[3]) for dx, dy, dz in block_order()]
    ).astype(jnp.int32)
    own_phase = phase_rows(order, angle[0].transpose(1, 0, 2), scale)
    ints = jnp.concatenate([dest[:, 0], start[None]])
    mate_ints = lax.ppermute(ints, "tile", mates())
    mate_kernel = lax.ppermute(own_kernel, "tile", mates())
    mate_phase = lax.ppermute(own_phase, "tile", mates())
    info = jnp.stack([core, ints[-1], mate_ints[-1]]).astype(jnp.int32)
    dests = jnp.stack([ints[:-1], mate_ints[:-1]])

    kept, taken = [], []
    for pieces in (first, last):
        keep, send = interpolate(info, pieces, own_kernel, mate_kernel)
        kept.append(keep)
        taken.append(lax.ppermute(send, "tile", mates()))
    sums = parent_sums(info, dests, own_phase, mate_phase, kept, taken)

    received = lax.all_to_all(sums, ("tile", "sub"), split_axis=0, concat_axis=0, tiled=True)
    received = received.reshape(tile_count // 2, 2, groups, STRIP, columns // 2)
    side = jnp.sum(received.astype(jnp.float32), axis=(0, 2)) / math.sqrt(tile_count)
    side = side.transpose(1, 0, 2).reshape(STRIP, columns)
    other = lax.ppermute(side, "sub", [(0, 1), (1, 0)])
    first_sub = lax.axis_index("sub") == 0
    return jnp.stack([jnp.where(first_sub, side, other), jnp.where(first_sub, other, side)])


def solution(mesh):
    placed = (
        P("sub", "tile", None, None, None),
        P("tile", None),
        P("tile", None),
        P("tile", None),
        P("tile"),
        P(),
        P("sub", None, None, "tile"),
        P("tile", None),
    )
    return jax.shard_map(
        local, mesh=mesh, in_specs=placed, out_specs=P(None, "tile", None), check_vma=False
    )
```

```python
import math

import jax
import jax.numpy as jnp
from jax import lax
from jax.experimental import pallas as pl
from jax.experimental.pallas import tpu as pltpu
from jax.sharding import PartitionSpec as P

STRIP = 16
PAD = 256
SIDES = (4, 2, 4, 2)
MIB = 1 << 20
MARK = jax.ShapeDtypeStruct((8, 128), jnp.int32)
START, SHIFT, CORE, DEST = 0, 1, 2, 8
RING = (0, -1, 1, 2)


def tile_at(x, y, z, core):
    return (((x % SIDES[0]) * SIDES[1] + y % SIDES[1]) * SIDES[2] + z % SIDES[2]) * SIDES[3] + core


def shifted(dx=0, dy=0, dz=0):
    return [
        (tile_at(x, y, z, c), tile_at(x + dx, y + dy, z + dz, c))
        for x in range(SIDES[0])
        for y in range(SIDES[1])
        for z in range(SIDES[2])
        for c in range(SIDES[3])
    ]


def mates():
    count = math.prod(SIDES)
    return [(i, i ^ 1) for i in range(count)]


def send(arrays, moves):
    return [lax.ppermute(array, "tile", move) for array, move in zip(arrays, moves)]


def rows_of(*arrays):
    return jnp.concatenate(arrays, 0)


def lanes_of(*arrays):
    return jnp.concatenate(arrays, 1)


def block_order(swap):
    places = [(a, 0, b) for b in (0, -1, 1) for a in RING] + [(a, 1, 0) for a in RING]
    places += [(a, 1, b) for b in (-1, 1) for a in RING]
    places += [(a, dy, 2) for half in (RING[:2], RING[2:]) for dy in (0, 1) for a in half]
    return [(b, dy, a) if swap else (a, dy, b) for a, dy, b in places]


def frame_kernel(ints, band_ref, raw_ref, mark_ref, out_ref, done_ref):
    held = 256
    rows = held - 16
    window, columns = raw_ref.shape
    total = out_ref.shape[0]
    done_ref[...] = jnp.zeros_like(done_ref)
    steps = lax.broadcasted_iota(jnp.int32, (rows, held), 1) - lax.broadcasted_iota(
        jnp.int32, (rows, held), 0
    )
    depth = lax.broadcasted_iota(jnp.int32, (rows, columns), 0)
    shift = ints[SHIFT]
    raised = (shift + 15) // 16 * 16
    low, high = band_ref[0:1, :], band_ref[1:2, :]
    for i in range(pl.cdiv(total, rows)):
        start = min(i * rows, total - rows)
        base = pl.multiple_of(jnp.clip(start - raised, 0, window - held), 16)
        move = jnp.where(steps == start - shift - base, 1.0, 0.0).astype(jnp.bfloat16)
        moved = jnp.dot(move, raw_ref[pl.ds(base, held), :], preferred_element_type=jnp.float32)
        first = start - shift
        moved = jnp.where((depth >= low - first) & (depth < high - first), moved, 0.0)
        out_ref[start : start + rows, :] = moved.astype(out_ref.dtype)


def fit_window(ints, bands, kernel, mark):
    window, columns = kernel.shape
    rows = window + PAD
    vmem = pl.BlockSpec(memory_space=pltpu.VMEM)
    return pl.pallas_call(
        frame_kernel,
        out_shape=(pltpu.VMEM((rows, columns), kernel.dtype), MARK),
        in_specs=[
            pl.BlockSpec(memory_space=pltpu.SMEM),
            vmem,
            vmem,
            pl.BlockSpec(memory_space=pl.ANY),
        ],
        out_specs=(vmem, vmem),
        compiler_params=pltpu.CompilerParams(vmem_limit_bytes=12 * MIB),
        cost_estimate=pl.CostEstimate(flops=rows * columns, bytes_accessed=columns, transcendentals=0),
        name="frame",
    )(ints, bands, kernel, mark)


def sine_cosine(angle):
    half = angle * 0.5
    square = half * half
    sine, cosine = jnp.float32(-1.0 / math.factorial(11)), jnp.float32(1.0 / math.factorial(12))
    for power in (9, 7, 5, 3, 1):
        sine = sine * square + jnp.float32((-1) ** (power // 2) / math.factorial(power))
    for power in (10, 8, 6, 4, 2, 0):
        cosine = cosine * square + jnp.float32((-1) ** (power // 2) / math.factorial(power))
    sine = sine * half
    return 2.0 * sine * cosine, 1.0 - 2.0 * sine * sine


def phase_kernel(order, angle_ref, *refs, scale):
    outs, done_ref = refs[:2], refs[2]
    done_ref[...] = jnp.zeros_like(done_ref)
    pulses, steps, rows = angle_ref.shape
    group = 128 // steps
    for swap in range(2):
        for core in range(SIDES[3]):
            for part, out_ref in enumerate(outs):
                first = ((swap * SIDES[3] + core) * len(outs) + part) * group
                picked = [angle_ref[order[first + i]] for i in range(group)]
                sine, cosine = sine_cosine(jnp.concatenate(picked, 0))
                at = (swap * SIDES[3] + core) * 128
                out_ref[swap, :, at : at + 128] = (cosine * scale).T.astype(out_ref.dtype)
                out_ref[1 - swap, :, at : at + 128] = (sine * scale).T.astype(out_ref.dtype)


def phase_rows(order, angle, scale):
    pulses, steps, rows = angle.shape
    depth = pulses * steps
    block = 128
    return pl.pallas_call(
        lambda *refs: phase_kernel(*refs, scale=scale),
        out_shape=(jax.ShapeDtypeStruct((2, rows, depth), jnp.bfloat16),) * 2 + (MARK,),
        grid_spec=pltpu.PrefetchScalarGridSpec(
            num_scalar_prefetch=1,
            grid=(rows // block,),
            in_specs=[pl.BlockSpec((pulses, steps, block), lambda i, order: (0, 0, i))],
            out_specs=[pl.BlockSpec((2, block, depth), lambda i, order: (0, i, 0))] * 2
            + [pl.BlockSpec(MARK.shape, lambda i, order: (0, 0))],
        ),
        compiler_params=pltpu.CompilerParams(vmem_limit_bytes=8 * MIB),
        cost_estimate=pl.CostEstimate(flops=8 * depth * rows, bytes_accessed=rows, transcendentals=0),
        name="phases",
    )(order, angle)


def interp_kernel(own_ints, mate_ints, mark_ref, *refs, spans):
    pieces = len(spans)
    parts, kernels = refs[:pieces], refs[pieces : pieces + 2]
    keep_ref, send_ref, rows_ref, sems = refs[pieces + 2 :]
    core = own_ints[CORE]
    count = rows_ref.shape[0] // 2
    depth, columns = kernels[0].shape
    half = columns // 2
    copies, at = [], 0
    for i, (piece, (first, size)) in enumerate(zip(parts, spans)):
        copies.append(
            pltpu.make_async_copy(
                piece.at[pl.ds(first, size)], rows_ref.at[pl.ds(at, size)], sems.at[i]
            )
        )
        at += size
    for copy in copies:
        copy.start()
    for copy in copies:
        copy.wait()

    for tile, kernel_ref in enumerate(kernels):
        start = pl.multiple_of((own_ints, mate_ints)[tile][START], 128)
        for side, out_ref in ((core, keep_ref), (1 - core, send_ref)):
            out = jnp.dot(
                rows_ref[:, pl.ds(start, depth)],
                kernel_ref[:, pl.ds(pl.multiple_of(side * half, 128), half)],
                preferred_element_type=jnp.float32,
            ).astype(out_ref.dtype)
            out_ref[0, :, tile * half : (tile + 1) * half] = out[:count]
            out_ref[1, :, tile * half : (tile + 1) * half] = out[count:]


def interpolate(ints, mark, real, imag, own, mate):
    pieces = real + imag
    spans = [(first, size) for _, first, size in pieces]
    count = sum(size for _, size in spans)
    samples = pieces[0][0].shape[1]
    depth, columns = own.shape
    out = jax.ShapeDtypeStruct((2, count // 2, columns), jnp.bfloat16)
    vmem = pl.BlockSpec(memory_space=pltpu.VMEM)
    return pl.pallas_call(
        lambda *refs: interp_kernel(*refs, spans=spans),
        out_shape=(out, out),
        in_specs=[pl.BlockSpec(memory_space=pltpu.SMEM)] * 2
        + [pl.BlockSpec(memory_space=pl.ANY)] * (1 + len(pieces))
        + [vmem, vmem],
        out_specs=(vmem, vmem),
        scratch_shapes=[
            pltpu.VMEM((count, samples), jnp.bfloat16),
            pltpu.SemaphoreType.DMA((len(pieces),)),
        ],
        compiler_params=pltpu.CompilerParams(vmem_limit_bytes=12 * MIB),
        cost_estimate=pl.CostEstimate(
            flops=4 * count * depth * columns // 10,
            bytes_accessed=count * samples // 10,
            transcendentals=0,
        ),
        name="interp",
    )(*ints, mark, *[array for array, _, _ in pieces], own, mate)


def image_kernel(own_ints, mate_ints, *refs, count, before):
    phases, kept, taken = refs[:2], refs[2 : 2 + count], refs[2 + count : 2 + 2 * count]
    total_in = refs[2 + 2 * count] if before else None
    out_ref, done_ref, top_ref, low_ref = refs[2 + 2 * count + before : 6 + 2 * count + before]
    total_ref = refs[-1] if before else out_ref
    done_ref[...] = jnp.zeros_like(done_ref)
    depth, half = top_ref.shape
    rows = phases[0].shape[1]
    core = own_ints[CORE]
    block = 256
    total_ref[...] = total_in[...] if before else jnp.zeros_like(total_ref)

    def lay(pieces, side, column):
        at = 0
        for piece in pieces:
            size = piece.shape[1]
            real = piece[0, :, column : column + half]
            imag = piece[1, :, column : column + half]
            real_rows = pl.ds(pl.multiple_of(side * (depth // 4) + at, 16), size)
            imag_rows = pl.ds(pl.multiple_of(side * (depth // 4) + at + depth // 2, 16), size)
            top_ref[real_rows, :] = real
            top_ref[imag_rows, :] = -imag
            low_ref[real_rows, :] = real
            low_ref[imag_rows, :] = imag
            at += size

    for tile, phase_ref in enumerate(phases):
        lay(kept, core, tile * half)
        lay(taken, 1 - core, (1 - tile) * half)
        for first in range(0, rows, block):
            for side, rhs_ref in enumerate((top_ref, low_ref)):
                image = jnp.dot(
                    phase_ref[side, first : first + block, :],
                    rhs_ref[...],
                    preferred_element_type=jnp.float32,
                )
                for strip in range(block // STRIP):
                    target = (own_ints, mate_ints)[tile][DEST + first // STRIP + strip]
                    at = pl.multiple_of(target * (2 * STRIP) + side * STRIP, STRIP)
                    total_ref[pl.ds(at, STRIP), :] += image[strip * STRIP : (strip + 1) * STRIP]
    if before:
        out_ref[...] = total_ref[...].astype(out_ref.dtype)


def parent_sums(ints, own_phase, mate_phase, kept, taken, total=None):
    _, rows, depth = own_phase.shape
    half = kept[0].shape[2] // 2
    before = total is not None
    vmem = pl.BlockSpec(memory_space=pltpu.VMEM)
    smem = pl.BlockSpec(memory_space=pltpu.SMEM)
    shape = (2 * rows, half)
    rhs = pltpu.VMEM((depth, half), jnp.bfloat16)
    operands = [own_phase, mate_phase, *kept, *taken] + ([total] if before else [])
    return pl.pallas_call(
        lambda *refs: image_kernel(*refs, count=len(kept), before=int(before)),
        out_shape=(
            jax.ShapeDtypeStruct(shape, jnp.bfloat16) if before else pltpu.VMEM(shape, jnp.float32),
            MARK,
        ),
        in_specs=[smem, smem] + [vmem] * len(operands),
        out_specs=(vmem, vmem),
        scratch_shapes=[rhs, rhs] + ([pltpu.VMEM(shape, jnp.float32)] if before else []),
        compiler_params=pltpu.CompilerParams(vmem_limit_bytes=12 * MIB),
        cost_estimate=pl.CostEstimate(
            flops=8 * rows * depth * half // 10,
            bytes_accessed=rows * depth,
            transcendentals=0,
        ),
        name="image",
    )(*ints, *operands)


def local(pulses, kernel, band_start, band_width, offset, owner, angle, dest):
    groups = lax.axis_size("sub")
    tile_count = lax.axis_size("tile")
    me = lax.axis_index("tile")
    core = me % SIDES[3]
    _, _, parts, pulse_count, samples = pulses.shape
    step_count = owner.shape[0]
    window, columns = kernel.shape
    depth = window + PAD
    scale = 1.0 / math.sqrt(pulse_count * step_count * groups)
    tie = lax.optimization_barrier
    up_x, down_x, up_z, down_z = shifted(dx=1), shifted(dx=-1), shifted(dz=1), shifted(dz=-1)
    ways = (up_x, down_x, up_z, down_z)

    start = jnp.minimum(offset[0] // 128 * 128, samples - depth)
    bands = jnp.concatenate([band_start, band_start + band_width], 0)
    meta = jnp.stack([start, offset[0] - start, core] + [jnp.zeros_like(core)] * (DEST - 3))
    own_ints = jnp.concatenate([meta.astype(jnp.int32), dest[:, 0]])
    mate_kernel = lax.ppermute(kernel, "tile", mates())
    mate_bands = lax.ppermute(bands, "tile", mates())
    mate_ints = lax.ppermute(own_ints, "tile", mates())
    ints = (own_ints, mate_ints)
    x, y, z = me // (SIDES[1] * SIDES[2] * SIDES[3]), me // (SIDES[2] * SIDES[3]), me // SIDES[3]
    order = jnp.stack(
        [
            tile_at(x + dx, y + dy, z + dz, c)
            for swap in (False, True)
            for c in range(SIDES[3])
            for dx, dy, dz in block_order(swap)
        ]
    ).astype(jnp.int32)

    blocks = pulses[0, 0].transpose(1, 0, 2)
    spread = lax.all_to_all(blocks, "tile", split_axis=0, concat_axis=0, tiled=True)
    mine = jnp.take(spread, owner, axis=0).transpose(1, 0, 2).reshape(parts * step_count, samples)
    *phase, phased = phase_rows(order, angle[0].transpose(1, 0, 2), scale)
    mine, phased, swapped = tie((mine, phased, mate_kernel[:16, :128]))

    n = step_count
    mid = samples // 2
    a, b = mine[:n], mine[n:]
    got = send((mine, a, a, b, b), (shifted(dy=1), *ways))
    got, a, b, bands, mate_bands = tie((got, a, b, bands, mate_bands))

    pa, pb = got[0][:n], got[0][n:]
    a_low, a_high, b_low, b_high = got[1:]
    out = (
        lanes_of(a_low[:, :mid], pa),
        lanes_of(a_high[:, mid:], pa),
        lanes_of(b_low[:, :mid], pb),
        lanes_of(b_high[:, mid:], pb),
    )
    got = send(out, ways)
    own_frame, framed = fit_window(own_ints, bands, kernel, swapped)
    got, mate_bands, framed = tie((got, mate_bands, framed))

    line_a = rows_of(a, a_low, a_high, lanes_of(got[0][:, :mid], got[1][:, :mid]))
    line_b = rows_of(b, b_low, b_high, lanes_of(got[2][:, :mid], got[3][:, :mid]))
    pa_low, pa_high, pb_low, pb_high = (array[:, mid:] for array in got)
    out = (rows_of(line_b, pa_low), line_b, rows_of(line_a, pb_low), line_a)
    got = send(out, ways)
    mate_frame, framed = fit_window(mate_ints, mate_bands, mate_kernel, framed)
    mate_phase = [lax.ppermute(half, "tile", mates()) for half in phase]
    got, line_a, line_b, framed = tie((got, line_a, line_b, framed))

    b_low_x, b_high_x, a_low_z, a_high_z = got
    next_a = rows_of(pa, pa_low, pa_high, b_low_x[4 * n :])
    next_b = rows_of(pb, pb_low, pb_high, a_low_z[4 * n :])
    got = send((next_b, next_b, next_a, next_a), ways)
    whole = 4 * n
    first = interpolate(
        ints,
        framed,
        [(array, 0, whole) for array in (line_a, a_low_z, a_high_z, next_a)],
        [(array, 0, whole) for array in (line_b, b_low_x, b_high_x, next_b)],
        own_frame,
        mate_frame,
    )
    got, first = tie((got, first))

    out = (
        rows_of(b_low_x[: 2 * n], got[0][: 2 * n]),
        rows_of(b_high_x[2 * n : 4 * n], got[1][2 * n :]),
        rows_of(a_low_z[: 2 * n], got[2][: 2 * n]),
        rows_of(a_high_z[2 * n : 4 * n], got[3][2 * n :]),
    )
    last = send(out, ways)
    taken = [lax.ppermute(first[1], "tile", mates())]
    total, summed = parent_sums(ints, phase[0], mate_phase[0], [first[0]], taken)
    second = interpolate(
        ints,
        phased,
        [(array, 0, whole) for array in got[2:]],
        [(array, 0, whole) for array in got[:2]],
        own_frame,
        mate_frame,
    )
    last, second, summed = tie((last, second, summed))

    taken = [lax.ppermute(second[1], "tile", mates())]
    third = interpolate(
        ints,
        summed,
        [(array, 0, whole) for array in last[2:]],
        [(array, 0, whole) for array in last[:2]],
        own_frame,
        mate_frame,
    )
    taken.append(lax.ppermute(third[1], "tile", mates()))
    kept = [second[0], third[0]]
    sums, _ = parent_sums(ints, phase[1], mate_phase[1], kept, taken, total)

    received = lax.all_to_all(
        sums.reshape(-1, STRIP, columns // 2), ("tile", "sub"), split_axis=0, concat_axis=0, tiled=True
    )
    received = received.reshape(tile_count // 2, 2, groups, STRIP, columns // 2)
    side = jnp.sum(received.astype(jnp.float32), axis=(0, 2)) / math.sqrt(tile_count)
    side = side.transpose(1, 0, 2).reshape(STRIP, columns)
    other = lax.ppermute(side, "sub", [(0, 1), (1, 0)])
    first_sub = lax.axis_index("sub") == 0
    return jnp.stack([jnp.where(first_sub, side, other), jnp.where(first_sub, other, side)])


def solution(mesh):
    placed = (
        P("sub", "tile", None, None, None),
        P("tile", None),
        P("tile", None),
        P("tile", None),
        P("tile"),
        P(),
        P("sub", None, None, "tile"),
        P("tile", None),
    )
    return jax.shard_map(
        local, mesh=mesh, in_specs=placed, out_specs=P(None, "tile", None), check_vma=False
    )
```

```python
import math

import jax
import jax.numpy as jnp
from jax import lax
from jax.experimental import pallas as pl
from jax.experimental.pallas import tpu as pltpu
from jax.sharding import PartitionSpec as P

STRIP = 16
PAD = 256
SIDES = (4, 2, 4, 2)
MIB = 1 << 20
MARK = jax.ShapeDtypeStruct((8, 128), jnp.int32)
START, SHIFT, CORE, DEST = 0, 1, 2, 8
RING = (0, -1, 1, 2)


def tile_at(x, y, z, core):
    return (((x % SIDES[0]) * SIDES[1] + y % SIDES[1]) * SIDES[2] + z % SIDES[2]) * SIDES[3] + core


def shifted(dx=0, dy=0, dz=0):
    return [
        (tile_at(x, y, z, c), tile_at(x + dx, y + dy, z + dz, c))
        for x in range(SIDES[0])
        for y in range(SIDES[1])
        for z in range(SIDES[2])
        for c in range(SIDES[3])
    ]


def mates():
    count = math.prod(SIDES)
    return [(i, i ^ 1) for i in range(count)]


def send(arrays, moves):
    return [lax.ppermute(array, "tile", move) for array, move in zip(arrays, moves)]


def rows_of(*arrays):
    return jnp.concatenate(arrays, 0)


def lanes_of(*arrays):
    return jnp.concatenate(arrays, 1)


def block_order(swap):
    places = [(a, 0, b) for b in (0, -1, 1) for a in RING] + [(a, 1, 0) for a in RING]
    places += [(a, 1, b) for b in (-1, 1) for a in RING]
    places += [(a, dy, 2) for half in (RING[:2], RING[2:]) for dy in (0, 1) for a in half]
    return [(b, dy, a) if swap else (a, dy, b) for a, dy, b in places]


def cut_kernel(pulses_ref, out_ref):
    parts, pulses, _ = pulses_ref.shape
    count, width = out_ref.shape
    pieces = count // (parts * pulses)
    stacked = jnp.concatenate(
        [pulses_ref[i, :, j * width : (j + 1) * width] for i in range(parts) for j in range(pieces)], 0
    )
    target = lax.broadcasted_iota(jnp.int32, (count, count), 0)
    source = lax.broadcasted_iota(jnp.int32, (count, count), 1)
    wanted = (target % (parts * pieces)) * pulses + target // (parts * pieces)
    move = jnp.where(source == wanted, 1.0, 0.0).astype(out_ref.dtype)
    moved = jnp.dot(move, stacked, preferred_element_type=jnp.float32)
    out_ref[...] = moved.astype(out_ref.dtype)


def cut_pulses(block):
    parts, pulses, samples = block.shape
    group, pieces = 16, 8
    rows = group * parts * pieces
    out = pl.pallas_call(
        cut_kernel,
        out_shape=jax.ShapeDtypeStruct((pulses * parts * pieces, samples // pieces), block.dtype),
        grid=(pulses // group,),
        in_specs=[pl.BlockSpec((parts, group, samples), lambda i: (0, i, 0))],
        out_specs=pl.BlockSpec((rows, samples // pieces), lambda i: (i, 0)),
        compiler_params=pltpu.CompilerParams(vmem_limit_bytes=16 * MIB),
        cost_estimate=pl.CostEstimate(
            flops=2 * rows * block.size, bytes_accessed=4 * block.size, transcendentals=0
        ),
        name="cut",
    )(block)
    return out.reshape(pulses, parts * pieces, samples // pieces)


def pick_kernel(owner, spread_ref, *refs):
    mine_ref, real_ref, imag_ref, held_ref, sems = refs[-5:]
    steps, rows, width = held_ref.shape
    copies = [
        pltpu.make_async_copy(spread_ref.at[owner[s]], held_ref.at[s], sems.at[s]) for s in range(steps)
    ]
    for copy in copies:
        copy.start()
    pieces = rows // 2
    count = steps * rows
    target = lax.broadcasted_iota(jnp.int32, (count, count), 0)
    source = lax.broadcasted_iota(jnp.int32, (count, count), 1)
    piece, part, step = target // (2 * steps), target // steps % 2, target % steps
    move = jnp.where(source == step * rows + part * pieces + piece, 1.0, 0.0).astype(mine_ref.dtype)
    for copy in copies:
        copy.wait()
    moved = jnp.dot(
        move, held_ref[...].reshape(count, width), preferred_element_type=jnp.float32
    )
    for j in range(pieces):
        lanes = slice(j * width, (j + 1) * width)
        at = j * 2 * steps
        mine_ref[:, lanes] = moved[at : at + 2 * steps].astype(mine_ref.dtype)
        real_ref[:, lanes] = moved[at : at + steps].astype(real_ref.dtype)
        imag_ref[:, lanes] = moved[at + steps : at + 2 * steps].astype(imag_ref.dtype)


def pick_owners(owner, spread, *marks):
    _, rows, width = spread.shape
    steps = owner.shape[0]
    samples = width * rows // 2
    vmem = pl.BlockSpec(memory_space=pltpu.VMEM)
    part = jax.ShapeDtypeStruct((steps, samples), spread.dtype)
    return pl.pallas_call(
        pick_kernel,
        out_shape=(jax.ShapeDtypeStruct((2 * steps, samples), spread.dtype), part, part),
        in_specs=[pl.BlockSpec(memory_space=pltpu.SMEM)]
        + [pl.BlockSpec(memory_space=pl.ANY)] * (1 + len(marks)),
        out_specs=(vmem, vmem, vmem),
        scratch_shapes=[
            pltpu.VMEM((steps, rows, width), spread.dtype),
            pltpu.SemaphoreType.DMA((steps,)),
        ],
        compiler_params=pltpu.CompilerParams(vmem_limit_bytes=8 * MIB),
        cost_estimate=pl.CostEstimate(flops=samples, bytes_accessed=samples, transcendentals=0),
        name="pick",
    )(owner, spread, *marks)


def frame_kernel(ints, band_ref, raw_ref, *refs):
    out_ref, done_ref = refs[-2:]
    held = 256
    rows = held - 16
    window, columns = raw_ref.shape
    total = out_ref.shape[0]
    done_ref[...] = jnp.zeros_like(done_ref)
    steps = lax.broadcasted_iota(jnp.int32, (rows, held), 1) - lax.broadcasted_iota(
        jnp.int32, (rows, held), 0
    )
    depth = lax.broadcasted_iota(jnp.int32, (rows, columns), 0)
    shift = ints[SHIFT]
    raised = (shift + 15) // 16 * 16
    low, high = band_ref[0:1, :], band_ref[1:2, :]
    for i in range(pl.cdiv(total, rows)):
        start = min(i * rows, total - rows)
        base = pl.multiple_of(jnp.clip(start - raised, 0, window - held), 16)
        move = jnp.where(steps == start - shift - base, 1.0, 0.0).astype(jnp.bfloat16)
        moved = jnp.dot(move, raw_ref[pl.ds(base, held), :], preferred_element_type=jnp.float32)
        first = start - shift
        moved = jnp.where((depth >= low - first) & (depth < high - first), moved, 0.0)
        out_ref[start : start + rows, :] = moved.astype(out_ref.dtype)


def fit_window(ints, bands, kernel, *marks):
    window, columns = kernel.shape
    rows = window + PAD
    vmem = pl.BlockSpec(memory_space=pltpu.VMEM)
    return pl.pallas_call(
        frame_kernel,
        out_shape=(pltpu.VMEM((rows, columns), kernel.dtype), MARK),
        in_specs=[
            pl.BlockSpec(memory_space=pltpu.SMEM),
            vmem,
            vmem,
            *[pl.BlockSpec(memory_space=pl.ANY)] * len(marks),
        ],
        out_specs=(vmem, vmem),
        compiler_params=pltpu.CompilerParams(vmem_limit_bytes=12 * MIB),
        cost_estimate=pl.CostEstimate(
            flops=4 * rows * columns * PAD, bytes_accessed=20 * rows * columns, transcendentals=0
        ),
        name="frame",
    )(ints, bands, kernel, *marks)


def sine_cosine(angle):
    half = angle * 0.5
    square = half * half
    sine, cosine = jnp.float32(-1.0 / math.factorial(11)), jnp.float32(1.0 / math.factorial(12))
    for power in (9, 7, 5, 3, 1):
        sine = sine * square + jnp.float32((-1) ** (power // 2) / math.factorial(power))
    for power in (10, 8, 6, 4, 2, 0):
        cosine = cosine * square + jnp.float32((-1) ** (power // 2) / math.factorial(power))
    sine = sine * half
    return 2.0 * sine * cosine, 1.0 - 2.0 * sine * sine


def phase_kernel(order, angle_ref, *refs, scale):
    outs, done_ref = refs[:2], refs[2]
    done_ref[...] = jnp.zeros_like(done_ref)
    pulses, steps, rows = angle_ref.shape
    group = 128 // steps
    for swap in range(2):
        for core in range(SIDES[3]):
            for part, out_ref in enumerate(outs):
                first = ((swap * SIDES[3] + core) * len(outs) + part) * group
                picked = [angle_ref[order[first + i]] for i in range(group)]
                sine, cosine = sine_cosine(jnp.concatenate(picked, 0))
                at = (swap * SIDES[3] + core) * 128
                out_ref[swap, :, at : at + 128] = (cosine * scale).T.astype(out_ref.dtype)
                out_ref[1 - swap, :, at : at + 128] = (sine * scale).T.astype(out_ref.dtype)


def phase_rows(order, angle, scale):
    pulses, steps, rows = angle.shape
    depth = pulses * steps
    block = 128
    return pl.pallas_call(
        lambda *refs: phase_kernel(*refs, scale=scale),
        out_shape=(jax.ShapeDtypeStruct((2, rows, depth), jnp.bfloat16),) * 2 + (MARK,),
        grid_spec=pltpu.PrefetchScalarGridSpec(
            num_scalar_prefetch=1,
            grid=(rows // block,),
            in_specs=[pl.BlockSpec((pulses, steps, block), lambda i, order: (0, 0, i))],
            out_specs=[pl.BlockSpec((2, block, depth), lambda i, order: (0, i, 0))] * 2
            + [pl.BlockSpec(MARK.shape, lambda i, order: (0, 0))],
        ),
        compiler_params=pltpu.CompilerParams(vmem_limit_bytes=8 * MIB),
        cost_estimate=pl.CostEstimate(flops=8 * depth * rows, bytes_accessed=rows, transcendentals=0),
        name="phases",
    )(order, angle)


def interp_kernel(own_ints, mate_ints, mark_ref, *refs, spans):
    pieces = len(spans)
    parts, kernels = refs[:pieces], refs[pieces : pieces + 2]
    keep_ref, send_ref, rows_ref, sems = refs[pieces + 2 :]
    core = own_ints[CORE]
    count = rows_ref.shape[0] // 2
    depth, columns = kernels[0].shape
    half = columns // 2
    copies, at = [], 0
    for i, (piece, (first, size)) in enumerate(zip(parts, spans)):
        copies.append(
            pltpu.make_async_copy(
                piece.at[pl.ds(first, size)], rows_ref.at[pl.ds(at, size)], sems.at[i]
            )
        )
        at += size
    for copy in copies:
        copy.start()
    for copy in copies:
        copy.wait()

    for tile, kernel_ref in enumerate(kernels):
        start = pl.multiple_of((own_ints, mate_ints)[tile][START], 128)
        for side, out_ref in ((core, keep_ref), (1 - core, send_ref)):
            out = jnp.dot(
                rows_ref[:, pl.ds(start, depth)],
                kernel_ref[:, pl.ds(pl.multiple_of(side * half, 128), half)],
                preferred_element_type=jnp.float32,
            ).astype(out_ref.dtype)
            out_ref[0, :, tile * half : (tile + 1) * half] = out[:count]
            out_ref[1, :, tile * half : (tile + 1) * half] = out[count:]


def interpolate(ints, mark, real, imag, own, mate):
    pieces = real + imag
    spans = [(first, size) for _, first, size in pieces]
    count = sum(size for _, size in spans)
    samples = pieces[0][0].shape[1]
    depth, columns = own.shape
    out = jax.ShapeDtypeStruct((2, count // 2, columns), jnp.bfloat16)
    vmem = pl.BlockSpec(memory_space=pltpu.VMEM)
    return pl.pallas_call(
        lambda *refs: interp_kernel(*refs, spans=spans),
        out_shape=(out, out),
        in_specs=[pl.BlockSpec(memory_space=pltpu.SMEM)] * 2
        + [pl.BlockSpec(memory_space=pl.ANY)] * (1 + len(pieces))
        + [vmem, vmem],
        out_specs=(vmem, vmem),
        scratch_shapes=[
            pltpu.VMEM((count, samples), jnp.bfloat16),
            pltpu.SemaphoreType.DMA((len(pieces),)),
        ],
        compiler_params=pltpu.CompilerParams(vmem_limit_bytes=12 * MIB),
        cost_estimate=pl.CostEstimate(
            flops=4 * count * depth * columns // 10,
            bytes_accessed=count * samples // 10,
            transcendentals=0,
        ),
        name="interp",
    )(*ints, mark, *[array for array, _, _ in pieces], own, mate)


def image_kernel(own_ints, mate_ints, *refs, count, before):
    phases, kept, taken = refs[:2], refs[2 : 2 + count], refs[2 + count : 2 + 2 * count]
    total_in = refs[2 + 2 * count] if before else None
    out_ref, done_ref, top_ref, low_ref = refs[2 + 2 * count + before : 6 + 2 * count + before]
    total_ref = refs[-1] if before else out_ref
    done_ref[...] = jnp.zeros_like(done_ref)
    depth, half = top_ref.shape
    rows = phases[0].shape[1]
    core = own_ints[CORE]
    block = 256
    total_ref[...] = total_in[...] if before else jnp.zeros_like(total_ref)

    def lay(pieces, side, column):
        at = 0
        for piece in pieces:
            size = piece.shape[1]
            real = piece[0, :, column : column + half]
            imag = piece[1, :, column : column + half]
            real_rows = pl.ds(pl.multiple_of(side * (depth // 4) + at, 16), size)
            imag_rows = pl.ds(pl.multiple_of(side * (depth // 4) + at + depth // 2, 16), size)
            top_ref[real_rows, :] = real
            top_ref[imag_rows, :] = -imag
            low_ref[real_rows, :] = real
            low_ref[imag_rows, :] = imag
            at += size

    for tile, phase_ref in enumerate(phases):
        lay(kept, core, tile * half)
        lay(taken, 1 - core, (1 - tile) * half)
        for first in range(0, rows, block):
            for side, rhs_ref in enumerate((top_ref, low_ref)):
                image = jnp.dot(
                    phase_ref[side, first : first + block, :],
                    rhs_ref[...],
                    preferred_element_type=jnp.float32,
                )
                for strip in range(block // STRIP):
                    target = (own_ints, mate_ints)[tile][DEST + first // STRIP + strip]
                    at = pl.multiple_of(target * (2 * STRIP) + side * STRIP, STRIP)
                    total_ref[pl.ds(at, STRIP), :] += image[strip * STRIP : (strip + 1) * STRIP]
    if before:
        out_ref[...] = total_ref[...].astype(out_ref.dtype)


def parent_sums(ints, own_phase, mate_phase, kept, taken, total=None):
    _, rows, depth = own_phase.shape
    half = kept[0].shape[2] // 2
    before = total is not None
    vmem = pl.BlockSpec(memory_space=pltpu.VMEM)
    smem = pl.BlockSpec(memory_space=pltpu.SMEM)
    shape = (2 * rows, half)
    rhs = pltpu.VMEM((depth, half), jnp.bfloat16)
    operands = [own_phase, mate_phase, *kept, *taken] + ([total] if before else [])
    return pl.pallas_call(
        lambda *refs: image_kernel(*refs, count=len(kept), before=int(before)),
        out_shape=(
            jax.ShapeDtypeStruct(shape, jnp.bfloat16) if before else pltpu.VMEM(shape, jnp.float32),
            MARK,
        ),
        in_specs=[smem, smem] + [vmem] * len(operands),
        out_specs=(vmem, vmem),
        scratch_shapes=[rhs, rhs] + ([pltpu.VMEM(shape, jnp.float32)] if before else []),
        compiler_params=pltpu.CompilerParams(vmem_limit_bytes=12 * MIB),
        cost_estimate=pl.CostEstimate(
            flops=8 * rows * depth * half // 10,
            bytes_accessed=rows * depth,
            transcendentals=0,
        ),
        name="image",
    )(*ints, *operands)


def local(pulses, kernel, band_start, band_width, offset, owner, angle, dest):
    groups = lax.axis_size("sub")
    tile_count = lax.axis_size("tile")
    me = lax.axis_index("tile")
    core = me % SIDES[3]
    _, _, parts, pulse_count, samples = pulses.shape
    step_count = owner.shape[0]
    window, columns = kernel.shape
    depth = window + PAD
    scale = 1.0 / math.sqrt(pulse_count * step_count * groups)
    tie = lax.optimization_barrier
    up_x, down_x, up_z, down_z = shifted(dx=1), shifted(dx=-1), shifted(dz=1), shifted(dz=-1)
    ways = (up_x, down_x, up_z, down_z)

    start = jnp.minimum(offset[0] // 128 * 128, samples - depth)
    bands = jnp.concatenate([band_start, band_start + band_width], 0)
    meta = jnp.stack([start, offset[0] - start, core] + [jnp.zeros_like(core)] * (DEST - 3))
    own_ints = jnp.concatenate([meta.astype(jnp.int32), dest[:, 0]])
    mate_kernel = lax.ppermute(kernel, "tile", mates())
    mate_bands = lax.ppermute(bands, "tile", mates())
    mate_ints = lax.ppermute(own_ints, "tile", mates())
    ints = (own_ints, mate_ints)
    x, y, z = me // (SIDES[1] * SIDES[2] * SIDES[3]), me // (SIDES[2] * SIDES[3]), me // SIDES[3]
    order = jnp.stack(
        [
            tile_at(x + dx, y + dy, z + dz, c)
            for swap in (False, True)
            for c in range(SIDES[3])
            for dx, dy, dz in block_order(swap)
        ]
    ).astype(jnp.int32)

    blocks = cut_pulses(pulses[0, 0])
    spread = lax.all_to_all(blocks, "tile", split_axis=0, concat_axis=0, tiled=True)
    *phase, phased = phase_rows(order, angle[0].transpose(1, 0, 2), scale)
    own_frame, framed = fit_window(own_ints, bands, kernel)
    mate_phase = [lax.ppermute(half, "tile", mates()) for half in phase]
    sent = [half[0, :16, :128] for half in mate_phase]
    mine, a, b = pick_owners(
        owner, spread, phased, framed, mate_kernel, mate_bands, mate_ints
    )

    n = step_count
    whole = 4 * n
    other, a_low, a_high, b_low, b_high, a_far, b_far = send(
        (mine, a, a, b, b, a, b), (shifted(dy=1), *ways, shifted(dx=2), shifted(dz=2))
    )
    pa, pb = other[:n], other[n:]
    line_a = rows_of(a, a_low, a_high, a_far, pb)
    line_b = rows_of(b, b_low, b_high, b_far, pa)
    far = rows_of(a_far, b_far)
    line_a, line_b, far, mate_bands = tie((line_a, line_b, far, mate_bands))

    got = send((line_b, line_b, line_a, line_a, far), (*ways, shifted(dy=1)))
    mate_frame, framed = fit_window(mate_ints, mate_bands, mate_kernel)
    got, line_a, line_b, framed = tie((got, line_a, line_b, framed))

    b_low_x, b_high_x, a_low_z, a_high_z, far = got
    pa_far, pb_far = far[:n], far[n:]
    next_a = rows_of(pa, b_low_x[whole:], b_high_x[whole:], pa_far)
    next_b = rows_of(pb, a_low_z[whole:], a_high_z[whole:], pb_far)
    got = send((next_b, next_b, next_a, next_a), ways)
    first = interpolate(
        ints,
        framed,
        [(array, 0, whole) for array in (line_a, a_low_z, a_high_z, next_a)],
        [(array, 0, whole) for array in (line_b, b_low_x, b_high_x, next_b)],
        own_frame,
        mate_frame,
    )
    got, first = tie((got, first))

    out = (
        rows_of(b_low_x[: 2 * n], got[0][: 2 * n]),
        rows_of(b_high_x[2 * n : 4 * n], got[1][2 * n :]),
        rows_of(a_low_z[: 2 * n], got[2][: 2 * n]),
        rows_of(a_high_z[2 * n : 4 * n], got[3][2 * n :]),
    )
    last = send(out, ways)
    taken = [lax.ppermute(first[1], "tile", mates())]
    total, summed = parent_sums(ints, phase[0], mate_phase[0], [first[0]], taken)
    second = interpolate(
        ints,
        framed,
        [(array, 0, whole) for array in got[2:]],
        [(array, 0, whole) for array in got[:2]],
        own_frame,
        mate_frame,
    )
    last, second, summed = tie((last, second, summed))

    taken = [lax.ppermute(second[1], "tile", mates())]
    third = interpolate(
        ints,
        summed,
        [(array, 0, whole) for array in last[2:]],
        [(array, 0, whole) for array in last[:2]],
        own_frame,
        mate_frame,
    )
    taken.append(lax.ppermute(third[1], "tile", mates()))
    kept = [second[0], third[0]]
    sums, _ = parent_sums(ints, phase[1], mate_phase[1], kept, taken, total)

    received = lax.all_to_all(
        sums.reshape(-1, STRIP, columns // 2), ("tile", "sub"), split_axis=0, concat_axis=0, tiled=True
    )
    received = received.reshape(tile_count // 2, 2, groups, STRIP, columns // 2)
    side = jnp.sum(received.astype(jnp.float32), axis=(0, 2)) / math.sqrt(tile_count)
    side = side.transpose(1, 0, 2).reshape(STRIP, columns)
    other = lax.ppermute(side, "sub", [(0, 1), (1, 0)])
    first_sub = lax.axis_index("sub") == 0
    return jnp.stack([jnp.where(first_sub, side, other), jnp.where(first_sub, other, side)])


def solution(mesh):
    placed = (
        P("sub", "tile", None, None, None),
        P("tile", None),
        P("tile", None),
        P("tile", None),
        P("tile"),
        P(),
        P("sub", None, None, "tile"),
        P("tile", None),
    )
    return jax.shard_map(
        local, mesh=mesh, in_specs=placed, out_specs=P(None, "tile", None), check_vma=False
    )
```

```python
import math

import jax
import jax.numpy as jnp
from jax import lax
from jax.experimental import pallas as pl
from jax.experimental.pallas import tpu as pltpu
from jax.sharding import PartitionSpec as P

STRIP = 16
PAD = 256
SIDES = (4, 2, 4, 2)
MIB = 1 << 20
MARK = jax.ShapeDtypeStruct((8, 128), jnp.int32)
START, SHIFT, CORE, DEST = 0, 1, 2, 8
RING = (0, -1, 1, 2)


def tile_at(x, y, z, core):
    return (((x % SIDES[0]) * SIDES[1] + y % SIDES[1]) * SIDES[2] + z % SIDES[2]) * SIDES[3] + core


def shifted(dy=0, first=0):
    return [
        (tile_at(x, y, z, c), tile_at(x + first * (c == 0), y + dy, z + first * (c == 1), c))
        for x in range(SIDES[0])
        for y in range(SIDES[1])
        for z in range(SIDES[2])
        for c in range(SIDES[3])
    ]


def crossed(first):
    return [
        (tile_at(x, y, z, c), tile_at(x + first * (c == 1), y, z + first * (c == 0), c))
        for x in range(SIDES[0])
        for y in range(SIDES[1])
        for z in range(SIDES[2])
        for c in range(SIDES[3])
    ]


def mates():
    count = math.prod(SIDES)
    return [(i, i ^ 1) for i in range(count)]


def send(arrays, moves):
    return [lax.ppermute(array, "tile", move) for array, move in zip(arrays, moves)]


def rows_of(*arrays):
    return jnp.concatenate(arrays, 0)


def block_order(swap):
    places = [(a, 0, b) for b in (0, -1, 1) for a in RING] + [(a, 1, 0) for a in RING]
    places += [(a, 1, b) for b in (-1, 1) for a in RING]
    places += [(a, dy, 2) for half in (RING[:2], RING[2:]) for dy in (0, 1) for a in half]
    return [(b, dy, a) if swap else (a, dy, b) for a, dy, b in places]


def cut_kernel(pulses_ref, out_ref):
    parts, pulses, _ = pulses_ref.shape
    count, width = out_ref.shape
    pieces = count // (parts * pulses)
    stacked = jnp.concatenate(
        [pulses_ref[i, :, j * width : (j + 1) * width] for i in range(parts) for j in range(pieces)], 0
    )
    target = lax.broadcasted_iota(jnp.int32, (count, count), 0)
    source = lax.broadcasted_iota(jnp.int32, (count, count), 1)
    piece, inner = target % pieces, target // pieces % 2
    part, pair = target // (2 * pieces) % parts, target // (2 * pieces * parts)
    wanted = (part * pieces + piece) * pulses + 2 * pair + inner
    move = jnp.where(source == wanted, 1.0, 0.0).astype(out_ref.dtype)
    moved = jnp.dot(move, stacked, preferred_element_type=jnp.float32)
    out_ref[...] = moved.astype(out_ref.dtype)


def cut_pulses(block):
    parts, pulses, samples = block.shape
    group, pieces = 16, 8
    rows = group * parts * pieces
    out = pl.pallas_call(
        cut_kernel,
        out_shape=jax.ShapeDtypeStruct((pulses * parts * pieces, samples // pieces), block.dtype),
        grid=(pulses // group,),
        in_specs=[pl.BlockSpec((parts, group, samples), lambda i: (0, i, 0))],
        out_specs=pl.BlockSpec((rows, samples // pieces), lambda i: (i, 0)),
        compiler_params=pltpu.CompilerParams(vmem_limit_bytes=16 * MIB),
        cost_estimate=pl.CostEstimate(
            flops=2 * rows * block.size, bytes_accessed=4 * block.size, transcendentals=0
        ),
        name="cut",
    )(block)
    return out.reshape(pulses, parts * pieces, samples // pieces)


def pick_kernel(owner, spread_ref, *refs):
    mine_ref, held_ref, sems = refs[-3:]
    steps, rows, width = held_ref.shape
    copies = [
        pltpu.make_async_copy(spread_ref.at[owner[s]], held_ref.at[s], sems.at[s]) for s in range(steps)
    ]
    for copy in copies:
        copy.start()
    pieces = rows // 2
    count = steps * rows
    target = lax.broadcasted_iota(jnp.int32, (count, count), 0)
    source = lax.broadcasted_iota(jnp.int32, (count, count), 1)
    piece, inner, step = target // (2 * steps), target // steps % 2, target % steps
    move = jnp.where(source == step * rows + inner * pieces + piece, 1.0, 0.0).astype(mine_ref.dtype)
    for copy in copies:
        copy.wait()
    moved = jnp.dot(
        move, held_ref[...].reshape(count, width), preferred_element_type=jnp.float32
    )
    for j in range(pieces):
        lanes = slice(j * width, (j + 1) * width)
        at = j * 2 * steps
        mine_ref[:, lanes] = moved[at : at + 2 * steps].astype(mine_ref.dtype)


def pick_owners(owner, spread, *marks):
    _, rows, width = spread.shape
    steps = owner.shape[0]
    samples = width * rows // 2
    vmem = pl.BlockSpec(memory_space=pltpu.VMEM)
    return pl.pallas_call(
        pick_kernel,
        out_shape=jax.ShapeDtypeStruct((2 * steps, samples), spread.dtype),
        in_specs=[pl.BlockSpec(memory_space=pltpu.SMEM)]
        + [pl.BlockSpec(memory_space=pl.ANY)] * (1 + len(marks)),
        out_specs=vmem,
        scratch_shapes=[
            pltpu.VMEM((steps, rows, width), spread.dtype),
            pltpu.SemaphoreType.DMA((steps,)),
        ],
        compiler_params=pltpu.CompilerParams(vmem_limit_bytes=8 * MIB),
        cost_estimate=pl.CostEstimate(flops=samples, bytes_accessed=samples, transcendentals=0),
        name="pick",
    )(owner, spread, *marks)


def frame_kernel(ints, band_ref, raw_ref, *refs):
    out_ref, done_ref = refs[-2:]
    held = 256
    rows = held - 16
    window, columns = raw_ref.shape
    total = out_ref.shape[0]
    done_ref[...] = jnp.zeros_like(done_ref)
    steps = lax.broadcasted_iota(jnp.int32, (rows, held), 1) - lax.broadcasted_iota(
        jnp.int32, (rows, held), 0
    )
    depth = lax.broadcasted_iota(jnp.int32, (rows, columns), 0)
    shift = ints[SHIFT]
    raised = (shift + 15) // 16 * 16
    low, high = band_ref[0:1, :], band_ref[1:2, :]
    for i in range(pl.cdiv(total, rows)):
        start = min(i * rows, total - rows)
        base = pl.multiple_of(jnp.clip(start - raised, 0, window - held), 16)
        move = jnp.where(steps == start - shift - base, 1.0, 0.0).astype(jnp.bfloat16)
        moved = jnp.dot(move, raw_ref[pl.ds(base, held), :], preferred_element_type=jnp.float32)
        first = start - shift
        moved = jnp.where((depth >= low - first) & (depth < high - first), moved, 0.0)
        out_ref[start : start + rows, :] = moved.astype(out_ref.dtype)


def fit_window(ints, bands, kernel, *marks):
    window, columns = kernel.shape
    rows = window + PAD
    vmem = pl.BlockSpec(memory_space=pltpu.VMEM)
    return pl.pallas_call(
        frame_kernel,
        out_shape=(pltpu.VMEM((rows, columns), kernel.dtype), MARK),
        in_specs=[
            pl.BlockSpec(memory_space=pltpu.SMEM),
            vmem,
            vmem,
            *[pl.BlockSpec(memory_space=pl.ANY)] * len(marks),
        ],
        out_specs=(vmem, vmem),
        compiler_params=pltpu.CompilerParams(vmem_limit_bytes=12 * MIB),
        cost_estimate=pl.CostEstimate(
            flops=4 * rows * columns * PAD, bytes_accessed=20 * rows * columns, transcendentals=0
        ),
        name="frame",
    )(ints, bands, kernel, *marks)


def sine_cosine(angle):
    half = angle * 0.5
    square = half * half
    sine, cosine = jnp.float32(-1.0 / math.factorial(11)), jnp.float32(1.0 / math.factorial(12))
    for power in (9, 7, 5, 3, 1):
        sine = sine * square + jnp.float32((-1) ** (power // 2) / math.factorial(power))
    for power in (10, 8, 6, 4, 2, 0):
        cosine = cosine * square + jnp.float32((-1) ** (power // 2) / math.factorial(power))
    sine = sine * half
    return 2.0 * sine * cosine, 1.0 - 2.0 * sine * sine


def phase_kernel(order, angle_ref, *refs, scale):
    outs, done_ref = refs[:2], refs[2]
    done_ref[...] = jnp.zeros_like(done_ref)
    pulses, steps, rows = angle_ref.shape
    group = 128 // steps
    for swap in range(2):
        for part, out_ref in enumerate(outs):
            for block in range(2):
                first = ((swap * len(outs) + part) * 2 + block) * group
                picked = [angle_ref[order[first + i]] for i in range(group)]
                sine, cosine = sine_cosine(jnp.concatenate(picked, 0))
                at = (swap * 2 + block) * 128
                out_ref[swap, :, at : at + 128] = (cosine * scale).T.astype(out_ref.dtype)
                out_ref[1 - swap, :, at : at + 128] = (sine * scale).T.astype(out_ref.dtype)


def phase_rows(order, angle, scale):
    pulses, steps, rows = angle.shape
    depth = pulses * steps
    block = 128
    return pl.pallas_call(
        lambda *refs: phase_kernel(*refs, scale=scale),
        out_shape=(jax.ShapeDtypeStruct((2, rows, depth), jnp.bfloat16),) * 2 + (MARK,),
        grid_spec=pltpu.PrefetchScalarGridSpec(
            num_scalar_prefetch=1,
            grid=(rows // block,),
            in_specs=[pl.BlockSpec((pulses, steps, block), lambda i, order: (0, 0, i))],
            out_specs=[pl.BlockSpec((2, block, depth), lambda i, order: (0, i, 0))] * 2
            + [pl.BlockSpec(MARK.shape, lambda i, order: (0, 0))],
        ),
        compiler_params=pltpu.CompilerParams(vmem_limit_bytes=8 * MIB),
        cost_estimate=pl.CostEstimate(flops=8 * depth * rows, bytes_accessed=rows, transcendentals=0),
        name="phases",
    )(order, angle)


def interp_kernel(own_ints, mate_ints, mark_ref, *refs, spans):
    pieces = len(spans)
    parts, kernels = refs[:pieces], refs[pieces : pieces + 2]
    keep_ref, send_ref, rows_ref, sems = refs[pieces + 2 :]
    core = own_ints[CORE]
    depth, columns = kernels[0].shape
    half = columns // 2
    copies, at = [], 0
    for i, (piece, (first, size)) in enumerate(zip(parts, spans)):
        copies.append(
            pltpu.make_async_copy(
                piece.at[pl.ds(first, size)], rows_ref.at[pl.ds(at, size)], sems.at[i]
            )
        )
        at += size
    for copy in copies:
        copy.start()
    for copy in copies:
        copy.wait()

    for tile, kernel_ref in enumerate(kernels):
        start = pl.multiple_of((own_ints, mate_ints)[tile][START], 128)
        for side, out_ref in ((core, keep_ref), (1 - core, send_ref)):
            out = jnp.dot(
                rows_ref[:, pl.ds(start, depth)],
                kernel_ref[:, pl.ds(pl.multiple_of(side * half, 128), half)],
                preferred_element_type=jnp.float32,
            ).astype(out_ref.dtype)
            out_ref[:, tile * half : (tile + 1) * half] = out


def interpolate(ints, mark, pieces, own, mate):
    spans = [(first, size) for _, first, size in pieces]
    count = sum(size for _, size in spans)
    samples = pieces[0][0].shape[1]
    depth, columns = own.shape
    out = jax.ShapeDtypeStruct((count, columns), jnp.bfloat16)
    vmem = pl.BlockSpec(memory_space=pltpu.VMEM)
    return pl.pallas_call(
        lambda *refs: interp_kernel(*refs, spans=spans),
        out_shape=(out, out),
        in_specs=[pl.BlockSpec(memory_space=pltpu.SMEM)] * 2
        + [pl.BlockSpec(memory_space=pl.ANY)] * (1 + len(pieces))
        + [vmem, vmem],
        out_specs=(vmem, vmem),
        scratch_shapes=[
            pltpu.VMEM((count, samples), jnp.bfloat16),
            pltpu.SemaphoreType.DMA((len(pieces),)),
        ],
        compiler_params=pltpu.CompilerParams(vmem_limit_bytes=12 * MIB),
        cost_estimate=pl.CostEstimate(
            flops=4 * count * depth * columns // 10,
            bytes_accessed=count * samples // 10,
            transcendentals=0,
        ),
        name="interp",
    )(*ints, mark, *[array for array, _, _ in pieces], own, mate)


def image_kernel(own_ints, mate_ints, *refs, count, before):
    phases, kept, taken = refs[:2], refs[2 : 2 + count], refs[2 + count : 2 + 2 * count]
    total_in = refs[2 + 2 * count] if before else None
    out_ref, done_ref, top_ref, low_ref = refs[2 + 2 * count + before : 6 + 2 * count + before]
    total_ref = refs[-1] if before else out_ref
    done_ref[...] = jnp.zeros_like(done_ref)
    depth, half = top_ref.shape
    rows = phases[0].shape[1]
    core = own_ints[CORE]
    block = 256
    total_ref[...] = total_in[...] if before else jnp.zeros_like(total_ref)

    def lay(pieces, side, column):
        at = pl.multiple_of(side * (depth // 2), 16)
        for piece in pieces:
            size = piece.shape[0]
            part = piece[:, column : column + half]
            top_ref[pl.ds(at, size), :] = jnp.where(side == 0, part, -part)
            low_ref[pl.ds(at, size), :] = part
            at = pl.multiple_of(at + size, 16)

    for tile, phase_ref in enumerate(phases):
        lay(kept, core, tile * half)
        lay(taken, 1 - core, (1 - tile) * half)
        for first in range(0, rows, block):
            for side, rhs_ref in enumerate((top_ref, low_ref)):
                image = jnp.dot(
                    phase_ref[side, first : first + block, :],
                    rhs_ref[...],
                    preferred_element_type=jnp.float32,
                )
                for strip in range(block // STRIP):
                    target = (own_ints, mate_ints)[tile][DEST + first // STRIP + strip]
                    at = pl.multiple_of(target * (2 * STRIP) + side * STRIP, STRIP)
                    total_ref[pl.ds(at, STRIP), :] += image[strip * STRIP : (strip + 1) * STRIP]
    if before:
        out_ref[...] = total_ref[...].astype(out_ref.dtype)


def parent_sums(ints, own_phase, mate_phase, kept, taken, total=None):
    _, rows, depth = own_phase.shape
    half = kept[0].shape[1] // 2
    before = total is not None
    vmem = pl.BlockSpec(memory_space=pltpu.VMEM)
    smem = pl.BlockSpec(memory_space=pltpu.SMEM)
    shape = (2 * rows, half)
    rhs = pltpu.VMEM((depth, half), jnp.bfloat16)
    operands = [own_phase, mate_phase, *kept, *taken] + ([total] if before else [])
    return pl.pallas_call(
        lambda *refs: image_kernel(*refs, count=len(kept), before=int(before)),
        out_shape=(
            jax.ShapeDtypeStruct(shape, jnp.bfloat16) if before else pltpu.VMEM(shape, jnp.float32),
            MARK,
        ),
        in_specs=[smem, smem] + [vmem] * len(operands),
        out_specs=(vmem, vmem),
        scratch_shapes=[rhs, rhs] + ([pltpu.VMEM(shape, jnp.float32)] if before else []),
        compiler_params=pltpu.CompilerParams(vmem_limit_bytes=12 * MIB),
        cost_estimate=pl.CostEstimate(
            flops=8 * rows * depth * half // 10,
            bytes_accessed=rows * depth,
            transcendentals=0,
        ),
        name="image",
    )(*ints, *operands)


def local(pulses, kernel, band_start, band_width, offset, owner, angle, dest):
    groups = lax.axis_size("sub")
    tile_count = lax.axis_size("tile")
    me = lax.axis_index("tile")
    core = me % SIDES[3]
    _, _, parts, pulse_count, samples = pulses.shape
    step_count = owner.shape[0]
    window, columns = kernel.shape
    depth = window + PAD
    scale = 1.0 / math.sqrt(pulse_count * step_count * groups)
    tie = lax.optimization_barrier

    start = jnp.minimum(offset[0] // 128 * 128, samples - depth)
    bands = jnp.concatenate([band_start, band_start + band_width], 0)
    meta = jnp.stack([start, offset[0] - start, core] + [jnp.zeros_like(core)] * (DEST - 3))
    own_ints = jnp.concatenate([meta.astype(jnp.int32), dest[:, 0]])
    mate_kernel = lax.ppermute(kernel, "tile", mates())
    mate_bands = lax.ppermute(bands, "tile", mates())
    mate_ints = lax.ppermute(own_ints, "tile", mates())
    ints = (own_ints, mate_ints)
    x, y, z = me // (SIDES[1] * SIDES[2] * SIDES[3]), me // (SIDES[2] * SIDES[3]), me // SIDES[3]
    order = jnp.stack(
        [
            tile_at(x + dx, y + dy, z + dz, c)
            for swap in (False, True)
            for dx, dy, dz in block_order(swap)
            for c in range(SIDES[3])
        ]
    ).astype(jnp.int32)

    blocks = cut_pulses(pulses[0, 0])
    spread = lax.all_to_all(blocks, "tile", split_axis=0, concat_axis=0, tiled=True)
    *phase, phased = phase_rows(order, angle[0].transpose(1, 0, 2), scale)
    own_frame, framed = fit_window(own_ints, bands, kernel)
    mate_phase = [lax.ppermute(half, "tile", mates()) for half in phase]
    sent = [half[0, :16, :128] for half in mate_phase]
    mine = pick_owners(
        owner, spread, phased, framed, mate_kernel, mate_bands, mate_ints
    )

    block = mine.shape[0]
    whole, two = 4 * block, 2 * block
    ways = (crossed(1), crossed(-1))
    other, low, high, far = send(
        (mine,) * 4, (shifted(dy=1), shifted(first=1), shifted(first=-1), shifted(first=2))
    )
    line = rows_of(mine, low, high, far)
    line, far, other, mate_bands = tie((line, far, other, mate_bands))

    low, high, far, other_low, other_high = send(
        (line, line, far, other, other),
        (*ways, shifted(dy=1), shifted(first=1), shifted(first=-1)),
    )
    mate_frame, framed = fit_window(mate_ints, mate_bands, mate_kernel)
    following = rows_of(other, other_low, other_high, far)
    low, high, line, following, framed = tie((low, high, line, following, framed))

    next_low, next_high = send((following, following), ways)
    first = interpolate(
        ints,
        framed,
        [(array, 0, whole) for array in (line, low, high, following)],
        own_frame,
        mate_frame,
    )
    next_low, next_high, first = tie((next_low, next_high, first))

    out = (rows_of(low[:two], next_low[:two]), rows_of(high[two:], next_high[two:]))
    last = send(out, ways)
    taken = [lax.ppermute(first[1], "tile", mates())]
    total, summed = parent_sums(ints, phase[0], mate_phase[0], [first[0]], taken)
    second = interpolate(
        ints, framed, [(array, 0, whole) for array in (next_low, next_high)], own_frame, mate_frame
    )
    last, second, summed = tie((last, second, summed))

    taken = [lax.ppermute(second[1], "tile", mates())]
    third = interpolate(ints, summed, [(array, 0, whole) for array in last], own_frame, mate_frame)
    taken.append(lax.ppermute(third[1], "tile", mates()))
    kept = [second[0], third[0]]
    sums, _ = parent_sums(ints, phase[1], mate_phase[1], kept, taken, total)

    received = lax.all_to_all(
        sums.reshape(-1, STRIP, columns // 2), ("tile", "sub"), split_axis=0, concat_axis=0, tiled=True
    )
    received = received.reshape(tile_count // 2, 2, groups, STRIP, columns // 2)
    side = jnp.sum(received.astype(jnp.float32), axis=(0, 2)) / math.sqrt(tile_count)
    side = side.transpose(1, 0, 2).reshape(STRIP, columns)
    other = lax.ppermute(side, "sub", [(0, 1), (1, 0)])
    first_sub = lax.axis_index("sub") == 0
    return jnp.stack([jnp.where(first_sub, side, other), jnp.where(first_sub, other, side)])


def solution(mesh):
    placed = (
        P("sub", "tile", None, None, None),
        P("tile", None),
        P("tile", None),
        P("tile", None),
        P("tile"),
        P(),
        P("sub", None, None, "tile"),
        P("tile", None),
    )
    return jax.shard_map(
        local, mesh=mesh, in_specs=placed, out_specs=P(None, "tile", None), check_vma=False
    )
```

```python
import math

import jax
import jax.numpy as jnp
from jax import lax
from jax.experimental import pallas as pl
from jax.experimental.pallas import tpu as pltpu
from jax.sharding import PartitionSpec as P

STRIP = 16
PAD = 256
SIDES = (4, 2, 4, 2)
MIB = 1 << 20
MARK = jax.ShapeDtypeStruct((8, 128), jnp.int32)
START, SHIFT, CORE, DEST = 0, 1, 2, 8
RING = (0, -1, 1, 2)


def tile_at(x, y, z, core):
    return (((x % SIDES[0]) * SIDES[1] + y % SIDES[1]) * SIDES[2] + z % SIDES[2]) * SIDES[3] + core


def shifted(dy=0, first=0):
    return [
        (tile_at(x, y, z, c), tile_at(x + first * (c == 0), y + dy, z + first * (c == 1), c))
        for x in range(SIDES[0])
        for y in range(SIDES[1])
        for z in range(SIDES[2])
        for c in range(SIDES[3])
    ]


def crossed(first):
    return [
        (tile_at(x, y, z, c), tile_at(x + first * (c == 1), y, z + first * (c == 0), c))
        for x in range(SIDES[0])
        for y in range(SIDES[1])
        for z in range(SIDES[2])
        for c in range(SIDES[3])
    ]


def mates():
    count = math.prod(SIDES)
    return [(i, i ^ 1) for i in range(count)]


def send(arrays, moves):
    return [lax.ppermute(array, "tile", move) for array, move in zip(arrays, moves)]


def rows_of(*arrays):
    return jnp.concatenate(arrays, 0)


def block_order(swap):
    places = [(a, 0, b) for b in (0, -1, 1) for a in RING] + [(a, 1, 0) for a in RING]
    places += [(a, 1, b) for b in (-1, 1) for a in RING]
    places += [(a, dy, 2) for dy in (0, 1) for a in RING]
    return [(b, dy, a) if swap else (a, dy, b) for a, dy, b in places]


def cut_kernel(pulses_ref, out_ref):
    parts, pulses, _ = pulses_ref.shape
    count, width = out_ref.shape
    pieces = count // (parts * pulses)
    stacked = jnp.concatenate(
        [pulses_ref[i, :, j * width : (j + 1) * width] for i in range(parts) for j in range(pieces)], 0
    )
    target = lax.broadcasted_iota(jnp.int32, (count, count), 0)
    source = lax.broadcasted_iota(jnp.int32, (count, count), 1)
    piece, inner = target % pieces, target // pieces % 2
    part, pair = target // (2 * pieces) % parts, target // (2 * pieces * parts)
    wanted = (part * pieces + piece) * pulses + 2 * pair + inner
    move = jnp.where(source == wanted, 1.0, 0.0).astype(out_ref.dtype)
    moved = jnp.dot(move, stacked, preferred_element_type=jnp.float32)
    out_ref[...] = moved.astype(out_ref.dtype)


def cut_pulses(block):
    parts, pulses, samples = block.shape
    group, pieces = 16, 8
    rows = group * parts * pieces
    out = pl.pallas_call(
        cut_kernel,
        out_shape=jax.ShapeDtypeStruct((pulses * parts * pieces, samples // pieces), block.dtype),
        grid=(pulses // group,),
        in_specs=[pl.BlockSpec((parts, group, samples), lambda i: (0, i, 0))],
        out_specs=pl.BlockSpec((rows, samples // pieces), lambda i: (i, 0)),
        compiler_params=pltpu.CompilerParams(vmem_limit_bytes=16 * MIB),
        cost_estimate=pl.CostEstimate(
            flops=2 * rows * block.size, bytes_accessed=4 * block.size, transcendentals=0
        ),
        name="cut",
    )(block)
    return out.reshape(pulses, parts * pieces, samples // pieces)


def pick_kernel(owner, spread_ref, *refs):
    mine_ref, held_ref, sems = refs[-3:]
    steps, rows, width = held_ref.shape
    copies = [
        pltpu.make_async_copy(spread_ref.at[owner[s]], held_ref.at[s], sems.at[s]) for s in range(steps)
    ]
    for copy in copies:
        copy.start()
    pieces = rows // 2
    count = steps * rows
    target = lax.broadcasted_iota(jnp.int32, (count, count), 0)
    source = lax.broadcasted_iota(jnp.int32, (count, count), 1)
    piece, inner, step = target // (2 * steps), target // steps % 2, target % steps
    move = jnp.where(source == step * rows + inner * pieces + piece, 1.0, 0.0).astype(mine_ref.dtype)
    for copy in copies:
        copy.wait()
    moved = jnp.dot(
        move, held_ref[...].reshape(count, width), preferred_element_type=jnp.float32
    )
    for j in range(pieces):
        lanes = slice(j * width, (j + 1) * width)
        at = j * 2 * steps
        mine_ref[:, lanes] = moved[at : at + 2 * steps].astype(mine_ref.dtype)


def pick_owners(owner, spread, *marks):
    _, rows, width = spread.shape
    steps = owner.shape[0]
    samples = width * rows // 2
    vmem = pl.BlockSpec(memory_space=pltpu.VMEM)
    return pl.pallas_call(
        pick_kernel,
        out_shape=jax.ShapeDtypeStruct((2 * steps, samples), spread.dtype),
        in_specs=[pl.BlockSpec(memory_space=pltpu.SMEM)]
        + [pl.BlockSpec(memory_space=pl.ANY)] * (1 + len(marks)),
        out_specs=vmem,
        scratch_shapes=[
            pltpu.VMEM((steps, rows, width), spread.dtype),
            pltpu.SemaphoreType.DMA((steps,)),
        ],
        compiler_params=pltpu.CompilerParams(vmem_limit_bytes=8 * MIB),
        cost_estimate=pl.CostEstimate(flops=samples, bytes_accessed=samples, transcendentals=0),
        name="pick",
    )(owner, spread, *marks)


def frame_kernel(ints, band_ref, raw_ref, *refs):
    out_ref, done_ref = refs[-2:]
    held = 256
    rows = held - 16
    window, columns = raw_ref.shape
    total = out_ref.shape[0]
    done_ref[...] = jnp.zeros_like(done_ref)
    steps = lax.broadcasted_iota(jnp.int32, (rows, held), 1) - lax.broadcasted_iota(
        jnp.int32, (rows, held), 0
    )
    depth = lax.broadcasted_iota(jnp.int32, (rows, columns), 0)
    shift = ints[SHIFT]
    raised = (shift + 15) // 16 * 16
    low, high = band_ref[0:1, :], band_ref[1:2, :]
    for i in range(pl.cdiv(total, rows)):
        start = min(i * rows, total - rows)
        base = pl.multiple_of(jnp.clip(start - raised, 0, window - held), 16)
        move = jnp.where(steps == start - shift - base, 1.0, 0.0).astype(jnp.bfloat16)
        moved = jnp.dot(move, raw_ref[pl.ds(base, held), :], preferred_element_type=jnp.float32)
        first = start - shift
        moved = jnp.where((depth >= low - first) & (depth < high - first), moved, 0.0)
        out_ref[start : start + rows, :] = moved.astype(out_ref.dtype)


def fit_window(ints, bands, kernel, *marks):
    window, columns = kernel.shape
    rows = window + PAD
    vmem = pl.BlockSpec(memory_space=pltpu.VMEM)
    return pl.pallas_call(
        frame_kernel,
        out_shape=(pltpu.VMEM((rows, columns), kernel.dtype), MARK),
        in_specs=[
            pl.BlockSpec(memory_space=pltpu.SMEM),
            vmem,
            vmem,
            *[pl.BlockSpec(memory_space=pl.ANY)] * len(marks),
        ],
        out_specs=(vmem, vmem),
        compiler_params=pltpu.CompilerParams(vmem_limit_bytes=12 * MIB),
        cost_estimate=pl.CostEstimate(
            flops=4 * rows * columns * PAD, bytes_accessed=20 * rows * columns, transcendentals=0
        ),
        name="frame",
    )(ints, bands, kernel, *marks)


def sine_cosine(angle):
    half = angle * 0.5
    square = half * half
    sine, cosine = jnp.float32(-1.0 / math.factorial(11)), jnp.float32(1.0 / math.factorial(12))
    for power in (9, 7, 5, 3, 1):
        sine = sine * square + jnp.float32((-1) ** (power // 2) / math.factorial(power))
    for power in (10, 8, 6, 4, 2, 0):
        cosine = cosine * square + jnp.float32((-1) ** (power // 2) / math.factorial(power))
    sine = sine * half
    return 2.0 * sine * cosine, 1.0 - 2.0 * sine * sine


def phase_kernel(order, angle_ref, *refs, scale):
    outs, done_ref = refs[:2], refs[2]
    done_ref[...] = jnp.zeros_like(done_ref)
    pulses, steps, rows = angle_ref.shape
    group = 128 // steps
    for swap in range(2):
        for part, out_ref in enumerate(outs):
            for block in range(2):
                first = ((swap * len(outs) + part) * 2 + block) * group
                picked = [angle_ref[order[first + i]] for i in range(group)]
                sine, cosine = sine_cosine(jnp.concatenate(picked, 0))
                at = (swap * 2 + block) * 128
                out_ref[swap, :, at : at + 128] = (cosine * scale).T.astype(out_ref.dtype)
                out_ref[1 - swap, :, at : at + 128] = (sine * scale).T.astype(out_ref.dtype)


def phase_rows(order, angle, scale):
    pulses, steps, rows = angle.shape
    depth = pulses * steps
    block = 128
    return pl.pallas_call(
        lambda *refs: phase_kernel(*refs, scale=scale),
        out_shape=(jax.ShapeDtypeStruct((2, rows, depth), jnp.bfloat16),) * 2 + (MARK,),
        grid_spec=pltpu.PrefetchScalarGridSpec(
            num_scalar_prefetch=1,
            grid=(rows // block,),
            in_specs=[pl.BlockSpec((pulses, steps, block), lambda i, order: (0, 0, i))],
            out_specs=[pl.BlockSpec((2, block, depth), lambda i, order: (0, i, 0))] * 2
            + [pl.BlockSpec(MARK.shape, lambda i, order: (0, 0))],
        ),
        compiler_params=pltpu.CompilerParams(vmem_limit_bytes=8 * MIB),
        cost_estimate=pl.CostEstimate(flops=8 * depth * rows, bytes_accessed=rows, transcendentals=0),
        name="phases",
    )(order, angle)


def interp_kernel(own_ints, mate_ints, mark_ref, *refs, spans):
    pieces = len(spans)
    parts, kernels = refs[:pieces], refs[pieces : pieces + 2]
    keep_ref, send_ref, rows_ref, sems = refs[pieces + 2 :]
    core = own_ints[CORE]
    depth, columns = kernels[0].shape
    half = columns // 2
    copies, at = [], 0
    for i, (piece, (first, size)) in enumerate(zip(parts, spans)):
        copies.append(
            pltpu.make_async_copy(
                piece.at[pl.ds(first, size)], rows_ref.at[pl.ds(at, size)], sems.at[i]
            )
        )
        at += size
    for copy in copies:
        copy.start()
    for copy in copies:
        copy.wait()

    for tile, kernel_ref in enumerate(kernels):
        start = pl.multiple_of((own_ints, mate_ints)[tile][START], 128)
        for side, out_ref in ((core, keep_ref), (1 - core, send_ref)):
            out = jnp.dot(
                rows_ref[:, pl.ds(start, depth)],
                kernel_ref[:, pl.ds(pl.multiple_of(side * half, 128), half)],
                preferred_element_type=jnp.float32,
            ).astype(out_ref.dtype)
            out_ref[:, tile * half : (tile + 1) * half] = out


def interpolate(ints, mark, pieces, own, mate):
    spans = [(first, size) for _, first, size in pieces]
    count = sum(size for _, size in spans)
    samples = pieces[0][0].shape[1]
    depth, columns = own.shape
    out = jax.ShapeDtypeStruct((count, columns), jnp.bfloat16)
    vmem = pl.BlockSpec(memory_space=pltpu.VMEM)
    return pl.pallas_call(
        lambda *refs: interp_kernel(*refs, spans=spans),
        out_shape=(out, out),
        in_specs=[pl.BlockSpec(memory_space=pltpu.SMEM)] * 2
        + [pl.BlockSpec(memory_space=pl.ANY)] * (1 + len(pieces))
        + [vmem, vmem],
        out_specs=(vmem, vmem),
        scratch_shapes=[
            pltpu.VMEM((count, samples), jnp.bfloat16),
            pltpu.SemaphoreType.DMA((len(pieces),)),
        ],
        compiler_params=pltpu.CompilerParams(vmem_limit_bytes=12 * MIB),
        cost_estimate=pl.CostEstimate(
            flops=4 * count * depth * columns // 10,
            bytes_accessed=count * samples // 10,
            transcendentals=0,
        ),
        name="interp",
    )(*ints, mark, *[array for array, _, _ in pieces], own, mate)


def image_kernel(own_ints, mate_ints, *refs, count, before):
    phases, kept, taken = refs[:2], refs[2 : 2 + count], refs[2 + count : 2 + 2 * count]
    total_in = refs[2 + 2 * count] if before else None
    out_ref, done_ref, top_ref, low_ref = refs[2 + 2 * count + before : 6 + 2 * count + before]
    total_ref = refs[-1] if before else out_ref
    done_ref[...] = jnp.zeros_like(done_ref)
    depth, half = top_ref.shape
    rows = phases[0].shape[1]
    core = own_ints[CORE]
    block = 256
    total_ref[...] = total_in[...] if before else jnp.zeros_like(total_ref)

    def lay(pieces, side, column):
        at = pl.multiple_of(side * (depth // 2), 16)
        for piece in pieces:
            size = piece.shape[0]
            part = piece[:, column : column + half]
            top_ref[pl.ds(at, size), :] = jnp.where(side == 0, part, -part)
            low_ref[pl.ds(at, size), :] = part
            at = pl.multiple_of(at + size, 16)

    for tile, phase_ref in enumerate(phases):
        lay(kept, core, tile * half)
        lay(taken, 1 - core, (1 - tile) * half)
        for first in range(0, rows, block):
            for side, rhs_ref in enumerate((top_ref, low_ref)):
                image = jnp.dot(
                    phase_ref[side, first : first + block, :],
                    rhs_ref[...],
                    preferred_element_type=jnp.float32,
                )
                for strip in range(block // STRIP):
                    target = (own_ints, mate_ints)[tile][DEST + first // STRIP + strip]
                    at = pl.multiple_of(target * (2 * STRIP) + side * STRIP, STRIP)
                    total_ref[pl.ds(at, STRIP), :] += image[strip * STRIP : (strip + 1) * STRIP]
    if before:
        out_ref[...] = total_ref[...].astype(out_ref.dtype)


def parent_sums(ints, own_phase, mate_phase, kept, taken, total=None):
    _, rows, depth = own_phase.shape
    half = kept[0].shape[1] // 2
    before = total is not None
    vmem = pl.BlockSpec(memory_space=pltpu.VMEM)
    smem = pl.BlockSpec(memory_space=pltpu.SMEM)
    shape = (2 * rows, half)
    rhs = pltpu.VMEM((depth, half), jnp.bfloat16)
    operands = [own_phase, mate_phase, *kept, *taken] + ([total] if before else [])
    return pl.pallas_call(
        lambda *refs: image_kernel(*refs, count=len(kept), before=int(before)),
        out_shape=(
            jax.ShapeDtypeStruct(shape, jnp.bfloat16) if before else pltpu.VMEM(shape, jnp.float32),
            MARK,
        ),
        in_specs=[smem, smem] + [vmem] * len(operands),
        out_specs=(vmem, vmem),
        scratch_shapes=[rhs, rhs] + ([pltpu.VMEM(shape, jnp.float32)] if before else []),
        compiler_params=pltpu.CompilerParams(vmem_limit_bytes=12 * MIB),
        cost_estimate=pl.CostEstimate(
            flops=8 * rows * depth * half // 10,
            bytes_accessed=rows * depth,
            transcendentals=0,
        ),
        name="image",
    )(*ints, *operands)


def local(pulses, kernel, band_start, band_width, offset, owner, angle, dest):
    groups = lax.axis_size("sub")
    tile_count = lax.axis_size("tile")
    me = lax.axis_index("tile")
    core = me % SIDES[3]
    _, _, parts, pulse_count, samples = pulses.shape
    step_count = owner.shape[0]
    window, columns = kernel.shape
    depth = window + PAD
    scale = 1.0 / math.sqrt(pulse_count * step_count * groups)
    tie = lax.optimization_barrier

    start = jnp.minimum(offset[0] // 128 * 128, samples - depth)
    bands = jnp.concatenate([band_start, band_start + band_width], 0)
    meta = jnp.stack([start, offset[0] - start, core] + [jnp.zeros_like(core)] * (DEST - 3))
    own_ints = jnp.concatenate([meta.astype(jnp.int32), dest[:, 0]])
    mate_kernel = lax.ppermute(kernel, "tile", mates())
    angle = angle[0].transpose(1, 0, 2)
    mate_angle = lax.ppermute(angle, "tile", mates())
    mate_bands = lax.ppermute(bands, "tile", mates())
    mate_ints = lax.ppermute(own_ints, "tile", mates())
    ints = (own_ints, mate_ints)
    x, y, z = me // (SIDES[1] * SIDES[2] * SIDES[3]), me // (SIDES[2] * SIDES[3]), me // SIDES[3]
    order = jnp.stack(
        [
            tile_at(x + dx, y + dy, z + dz, c)
            for swap in (False, True)
            for dx, dy, dz in block_order(swap)
            for c in range(SIDES[3])
        ]
    ).astype(jnp.int32)

    blocks = cut_pulses(pulses[0, 0])
    spread = lax.all_to_all(blocks, "tile", split_axis=0, concat_axis=0, tiled=True)
    *phase, phased = phase_rows(order, angle, scale)
    own_frame, framed = fit_window(own_ints, bands, kernel)
    mine = pick_owners(
        owner, spread, phased, framed, mate_kernel, mate_bands, mate_ints
    )

    block = mine.shape[0]
    whole, two = 4 * block, 2 * block
    ways = (crossed(1), crossed(-1))
    other, low, high, far = send(
        (mine,) * 4, (shifted(dy=1), shifted(first=1), shifted(first=-1), shifted(first=2))
    )
    line = rows_of(mine, low, high, far)
    line, far, other, mate_bands, sent = tie((line, far, other, mate_bands, mate_angle[0, :, :128]))

    low, high, far, other_low, other_high = send(
        (line, line, far, other, other),
        (*ways, shifted(dy=1), shifted(first=1), shifted(first=-1)),
    )
    mate_frame, framed = fit_window(mate_ints, mate_bands, mate_kernel, sent)
    following = rows_of(other, other_low, other_high, far)
    low, high, line, following, framed, order = tie((low, high, line, following, framed, order))

    next_low, next_high = send((following, following), ways)
    far = send((low[:two], high[two:]), ways)
    first = interpolate(
        ints,
        framed,
        [(array, 0, whole) for array in (line, low, high, following)],
        own_frame,
        mate_frame,
    )
    *mate_phase, mate_phased = phase_rows(order, mate_angle, scale)
    next_low, next_high, first, mate_phased = tie((next_low, next_high, first, mate_phased))

    last = send((next_low[:two], next_high[two:]), ways)
    taken = [lax.ppermute(first[1], "tile", mates())]
    total, summed = parent_sums(ints, phase[0], mate_phase[0], [first[0]], taken)
    second = interpolate(
        ints,
        mate_phased,
        [(array, 0, array.shape[0]) for array in (next_low, next_high, *far)],
        own_frame,
        mate_frame,
    )
    last, second, summed = tie((last, second, summed))

    taken = [lax.ppermute(second[1], "tile", mates())]
    third = interpolate(ints, summed, [(array, 0, two) for array in last], own_frame, mate_frame)
    taken.append(lax.ppermute(third[1], "tile", mates()))
    kept = [second[0], third[0]]
    sums, _ = parent_sums(ints, phase[1], mate_phase[1], kept, taken, total)

    received = lax.all_to_all(
        sums.reshape(-1, STRIP, columns // 2), ("tile", "sub"), split_axis=0, concat_axis=0, tiled=True
    )
    received = received.reshape(tile_count // 2, 2, groups, STRIP, columns // 2)
    side = jnp.sum(received.astype(jnp.float32), axis=(0, 2)) / math.sqrt(tile_count)
    side = side.transpose(1, 0, 2).reshape(STRIP, columns)
    other = lax.ppermute(side, "sub", [(0, 1), (1, 0)])
    first_sub = lax.axis_index("sub") == 0
    return jnp.stack([jnp.where(first_sub, side, other), jnp.where(first_sub, other, side)])


def solution(mesh):
    placed = (
        P("sub", "tile", None, None, None),
        P("tile", None),
        P("tile", None),
        P("tile", None),
        P("tile"),
        P(),
        P("sub", None, None, "tile"),
        P("tile", None),
    )
    return jax.shard_map(
        local, mesh=mesh, in_specs=placed, out_specs=P(None, "tile", None), check_vma=False
    )
```
